512 devices in a mesh: rep: 32 (over x, z), outer: 8 (over y), tp: 2 (over core).
Axes of the slice: x: 4, y: 8, z: 8, core: 2. Of those that a mesh axis runs over, the one named last changes fastest.
Arguments:
- activations: bfloat16 [8, 32, 128, 8192], P('outer', 'rep'), may hold values from -6 to 6
- kv_grads: bfloat16 [8, 32, 128, 2048], P('outer', 'rep', None, 'tp'), may hold values from -0.119628906 to 0.119628906
- kept_blocks: int32 [8, 32, 2, 1024], P('outer', 'rep', 'tp'), may hold values from 0 to 65535, as said below
- region_bounds: int32 [33], replicated, may hold values from 0 to 65536, as said below
- region_keep: int32 [32, 256], P('rep'), may hold values from 0 to 2303, as said below
- residual: float32 [8, 32, 2304, 256], P('outer', 'rep', None, 'tp'), may hold values from -6 to 6
Outputs:
- merged: float32 [32, 256, 256], P('rep', 'outer', 'tp')
- new_residual: float32 [8, 32, 2304, 256], P('outer', 'rep', None, 'tp')
The draws below stay inside these ranges and needn't reach their ends.
Inputs may be any that keep to these rules, and one draw needn't show every extreme that they name: `kept_blocks`: ids of one list are distinct. Of one replica's list for one column half, at most 64 fall in one region, exactly 64 in some region, and there is a region that receives exactly 64 from every replica and half. `region_bounds`: rising from 0 to 65536; every region holds 1792 to 2304 blocks, one exactly 2304. `region_keep`: distinct slots of each region, below the region's length.
All inputs are finite; a program needn't handle non-finite values.
Results may differ from the reference program's by a relative error of at most 0.002.
Values sent between devices are 32-bit elements; how exact they have to be, the bound alone decides.
No kernel may reach another device: no remote copies, remote signals or barrier semaphores. Data moves between devices by JAX's collectives and lax.ppermute only.
A program may use at most 128 MiB of HBM per device.

```python
import jax
import jax.numpy as jnp
from jax import lax

D = 8192
KV = 2048
HEAD = 128
TOK_DEV = 128
CAP = 64
KEEP2 = 256
NBLK = 65536
AVG = 2048
SPREAD = 256
RMAX = 2304
KEEP = 1024
N_REP = 32
N_OUTER = 8
N_TP = 2


def region_layout(key):
    first_key, second_key = jax.random.split(jax.random.fold_in(key, 7))
    shuffle = jax.random.permutation(first_key, N_REP)
    widened = jax.random.randint(second_key, (N_REP // 2,), 0, SPREAD + 1).at[0].set(SPREAD)
    change = jnp.zeros((N_REP,), jnp.int32).at[shuffle[0::2]].set(widened).at[shuffle[1::2]].set(-widened)
    lengths = AVG + change
    bounds = jnp.concatenate([jnp.zeros((1,), jnp.int32), jnp.cumsum(lengths).astype(jnp.int32)])
    return bounds


def draw_region_bounds(key, part):
    return region_layout(key)


def draw_kept_blocks(key, part):
    bounds = region_layout(key)
    starts = bounds[:-1]
    lengths = bounds[1:] - starts
    shortest = AVG - SPREAD
    half_cap = CAP // 2
    full_owner = jax.random.randint(jax.random.fold_in(key, 11), (), 0, N_REP)
    dev_keys = jax.random.split(jax.random.fold_in(key, 13), N_OUTER * N_REP * N_TP)

    def per_device(sub_key):
        key_a, key_b, key_c, key_d, key_e = jax.random.split(sub_key, 5)
        shuffle = jax.random.permutation(key_a, N_REP)
        where_full = jnp.argmax((shuffle == full_owner).astype(jnp.int32))
        shuffle = shuffle.at[where_full].set(shuffle[0]).at[0].set(full_owner)
        widened = jax.random.randint(key_b, (N_REP // 2,), 0, half_cap + 1).at[0].set(half_cap)
        counts = jnp.zeros((N_REP,), jnp.int32).at[shuffle[0::2]].set(half_cap + widened).at[shuffle[1::2]].set(half_cap - widened)
        spare_len = lengths - shortest
        offset_shift = jax.random.randint(key_c, (N_REP,), 0, 2 * SPREAD + 1) % (spare_len + 1)
        picked_offs = jax.vmap(lambda inner_key: jax.random.permutation(inner_key, shortest)[:CAP])(jax.random.split(key_d, N_REP))
        candidates = (starts[:, None] + offset_shift[:, None] + picked_offs).reshape(-1)
        live_mask = (jnp.arange(CAP)[None, :] < counts[:, None]).reshape(-1).astype(jnp.int32)
        order_idx = jnp.argsort(-live_mask, stable=True)[:KEEP]
        return jax.random.permutation(key_e, candidates[order_idx]).astype(jnp.int32)
    return jax.vmap(per_device)(dev_keys).reshape(N_OUTER, N_REP, N_TP, KEEP)


def draw_region_keep(key, part):
    bounds = region_layout(key)
    lengths = bounds[1:] - bounds[:-1]
    shortest = AVG - SPREAD
    many_keys = jax.random.split(jax.random.fold_in(key, 17), N_REP + 1)
    picked_offs = jax.vmap(lambda inner_key: jax.random.permutation(inner_key, shortest)[:KEEP2])(many_keys[:N_REP])
    offset_shift = jax.random.randint(many_keys[N_REP], (N_REP,), 0, 2 * SPREAD + 1) % (lengths - shortest + 1)
    return (picked_offs + offset_shift[:, None]).astype(jnp.int32)


def level_of(rng, shape, cuts, least, high):
    def one(dim, shards_of):
        steps = jax.random.uniform(jax.random.fold_in(jax.random.fold_in(rng, 6), dim), (shards_of,), jnp.float32, least / len(cuts), high / len(cuts))
        return jnp.repeat(jnp.exp(steps), shape[dim] // shards_of).reshape((-1,) + (1,) * (len(shape) - dim - 1))

    gain = one(*cuts[0])
    for cut in cuts[1:]:
        gain = gain * one(*cut)
    return gain


def noise(own_key, dims, scale, bound, shards=(), kind=jnp.bfloat16):
    gain = level_of(own_key, dims, shards, -0.22, 0.18) if shards else 1.0
    result = jax.random.normal(own_key, dims, jnp.float32) * scale * gain
    return jnp.minimum(jnp.maximum(result, -bound), bound).astype(kind)


def setup_inputs(seed: int = 0) -> dict:
    splits = jax.random.split(jax.random.key(seed), 7)
    return {
        "activations": noise(splits[0], (N_OUTER, N_REP, TOK_DEV, D), 1.0, 6.0, ((0, 8), (1, 32))),
        "kv_grads": noise(splits[1], (N_OUTER, N_REP, TOK_DEV, KV), 0.02, 0.119628906, ((0, 8), (1, 32), (3, 2))),
        "kept_blocks": draw_kept_blocks(jax.random.fold_in(splits[6], 71), 0),
        "region_bounds": draw_region_bounds(jax.random.fold_in(splits[6], 71), 0),
        "region_keep": draw_region_keep(jax.random.fold_in(splits[6], 71), 0),
        "residual": noise(splits[5], (N_OUTER, N_REP, RMAX, N_TP * HEAD), 1.0, 6.0, ((0, 8), (1, 32), (3, 2)), jnp.float32),
    }


def device_values(operands):
    inputs, grad_cols, block_ids = operands
    column_blocks = KV // (N_TP * HEAD)
    halves = grad_cols.reshape(TOK_DEV, N_TP * column_blocks, HEAD)
    results = []
    for half_index in range(N_TP):
        row_ids = block_ids[half_index] // column_blocks
        col_ids = half_index * column_blocks + block_ids[half_index] % column_blocks
        gathered = jnp.take(inputs, row_ids, axis=1).astype(jnp.float32)
        key_blocks = jnp.take(halves, col_ids, axis=1).astype(jnp.float32)
        results.append(jnp.einsum("tk,tkc->kc", gathered, key_blocks, precision=lax.Precision.HIGHEST))
    return jnp.stack(results)


def reference(activations, kv_grads, kept_blocks, region_bounds, region_keep, residual):
    devices = N_OUTER * N_REP
    all_values = lax.map(device_values, (activations.reshape(devices, TOK_DEV, D), kv_grads.reshape(devices, TOK_DEV, KV), kept_blocks.reshape(devices, N_TP, KEEP)))
    all_values = all_values.reshape(N_OUTER, N_REP, N_TP, KEEP, HEAD)
    starts = region_bounds[:-1]
    lengths = region_bounds[1:] - starts
    slot_ids = jnp.arange(RMAX, dtype=jnp.int32)
    inside_mask = slot_ids[None, :] < lengths[:, None]
    positions = jnp.where(inside_mask, starts[:, None] + slot_ids[None, :], 0).astype(jnp.int32)
    region_rows = jnp.arange(N_REP, dtype=jnp.int32)[:, None]
    kept_mask = jnp.zeros((N_REP, RMAX), jnp.bool_).at[region_rows, region_keep].set(True)
    keep_where = inside_mask & jnp.logical_not(kept_mask)
    merged_halves = []
    residual_halves = []
    for half_index in range(N_TP):
        merged = jnp.zeros((N_REP, KEEP2, HEAD), jnp.float32)
        refreshed = []
        for pod_index in range(N_OUTER):
            summed = jnp.zeros((NBLK, HEAD), jnp.float32).at[kept_blocks[pod_index, :, half_index].reshape(-1)].add(all_values[pod_index, :, half_index].reshape(-1, HEAD))
            totals = summed[positions] + residual[pod_index, :, :, half_index * HEAD:(half_index + 1) * HEAD]
            merged = merged + jnp.take_along_axis(totals, region_keep[:, :, None], axis=1)
            refreshed.append(jnp.where(keep_where[:, :, None], totals, jnp.zeros_like(totals)))
        merged_halves.append(merged)
        residual_halves.append(jnp.stack(refreshed))
    return jnp.concatenate(merged_halves, axis=2), jnp.concatenate(residual_halves, axis=3)
```

```python
import functools

import jax
import jax.numpy as jnp
from jax import lax
from jax.experimental import pallas as pl
from jax.experimental.pallas import tpu as pltpu
from jax.sharding import PartitionSpec as P

HEAD = 128
CAP = 64
LANES = 128
SLOT_TILE = 256
MIB = 1 << 20
CONTRACT_LAST = (((1,), (1,)), ((), ()))


def contract_last(left, right):
    return lax.dot_general(left, right, CONTRACT_LAST, preferred_element_type=jnp.float32)


def send_kernel(band, batch, bounds_ref, ids_ref, act_ref, grad_ref, out_ref):
    regions = bounds_ref.shape[0] - 1
    keep_count = ids_ref.shape[1]
    width = act_ref.shape[1]
    column_blocks = grad_ref.shape[1] // HEAD
    column_bits = column_blocks.bit_length() - 1
    chunks = keep_count // LANES
    stride = CAP + 1

    region_row = lax.broadcasted_iota(jnp.int32, (regions, LANES), 0)
    starts = jnp.zeros((regions, LANES), jnp.int32)
    ends = jnp.zeros((regions, LANES), jnp.int32)
    for region in range(regions):
        starts = jnp.where(region_row == region, bounds_ref[region], starts)
        ends = jnp.where(region_row == region, bounds_ref[region + 1], ends)

    ids = [ids_ref[:, c * LANES : (c + 1) * LANES] for c in range(chunks)]
    owned = [(i >= starts) & (i < ends) for i in ids]
    owned_f = [jnp.where(o, 1.0, 0.0) for o in owned]
    stacked = jnp.concatenate(owned_f, axis=0).astype(jnp.bfloat16)
    before = lax.broadcasted_iota(jnp.int32, (LANES, 2 * LANES), 0)
    after = lax.broadcasted_iota(jnp.int32, (LANES, 2 * LANES), 1)
    ladder = jnp.where((before < after) | (after >= LANES), 1.0, 0.0).astype(jnp.bfloat16)
    counted = jnp.dot(stacked, ladder, preferred_element_type=jnp.float32)
    running = jnp.zeros((regions, LANES), jnp.float32)
    rank_row = lax.broadcasted_iota(jnp.int32, (2 * CAP, LANES), 0) & (CAP - 1)
    ranked, high_part, low_part = [], [], []
    for c in range(chunks):
        rows = slice(c * regions, (c + 1) * regions)
        here = counted[rows, :LANES] + running
        running = running + counted[rows, LANES:]
        rank = jnp.sum(owned_f[c] * here, axis=0, keepdims=True).astype(jnp.int32)
        ranked.append(jnp.where(rank_row == rank, 1.0, 0.0).astype(jnp.bfloat16))
        code = ids[c] + 1
        high_part.append((owned_f[c] * (code >> 8).astype(jnp.float32)).astype(jnp.bfloat16))
        low_part.append((owned_f[c] * (code & 255).astype(jnp.float32)).astype(jnp.bfloat16))
    ranked = jnp.concatenate(ranked, axis=1)
    high_part = jnp.concatenate(high_part, axis=1)
    low_part = jnp.concatenate(low_part, axis=1)
    by_region = 256.0 * contract_last(high_part, ranked) + contract_last(low_part, ranked) - 1.0
    ranked = ranked[:CAP]
    by_rank = 256.0 * contract_last(ranked, high_part) + contract_last(ranked, low_part) - 1.0
    offsets = jnp.where(by_region < 0.0, -1.0, by_region - starts.astype(jnp.float32))

    lane = lax.broadcasted_iota(jnp.int32, (CAP, LANES), 1)
    grads = grad_ref[...]
    for first in range(0, regions, batch):
        columns, picked = [], []
        for region in range(first, first + batch):
            wanted = jnp.broadcast_to(by_rank[:, region : region + 1], (CAP, LANES)).astype(jnp.int32)
            base = (bounds_ref[region] >> column_bits) & ~(LANES - 1)
            base = pl.multiple_of(jnp.minimum(base, width - band), LANES)
            place = (wanted >> column_bits) - base
            columns.append(wanted & (column_blocks - 1))
            chosen = jnp.concatenate(
                [
                    jnp.where(lane + part == place, 1.0, 0.0).astype(jnp.bfloat16)
                    for part in range(0, band, LANES)
                ],
                axis=1,
            )
            picked.append(contract_last(chosen, act_ref[:, pl.ds(base, band)]).astype(jnp.bfloat16))
        columns = jnp.concatenate(columns, axis=0)
        wide = jnp.dot(jnp.concatenate(picked, axis=0), grads, preferred_element_type=jnp.float32)
        block = wide[:, :HEAD]
        for column in range(1, column_blocks):
            block = jnp.where(columns == column, wide[:, column * HEAD : (column + 1) * HEAD], block)
        for step in range(batch):
            region = first + step
            out_ref[region * stride : region * stride + CAP, :] = block[step * CAP : (step + 1) * CAP]
            out_ref[region * stride + CAP : (region + 1) * stride, :] = offsets[region : region + 1]


def send_rows(region_bounds, block_ids, inputs, grad_cols, band):
    regions = region_bounds.shape[0] - 1
    vmem = pl.BlockSpec(memory_space=pltpu.VMEM)
    return pl.pallas_call(
        functools.partial(send_kernel, band, 4),
        out_shape=jax.ShapeDtypeStruct((regions * (CAP + 1), HEAD), jnp.float32),
        in_specs=[pl.BlockSpec(memory_space=pltpu.SMEM), vmem, vmem, vmem],
        out_specs=vmem,
        compiler_params=pltpu.CompilerParams(vmem_limit_bytes=24 * MIB),
        cost_estimate=pl.CostEstimate(flops=10**9, bytes_accessed=4 * MIB, transcendentals=0),
        name="send_rows",
    )(region_bounds, block_ids, inputs, grad_cols)


def keep_kernel(slots_ref, keep_ref, residual_ref, column_ref, rows_ref):
    count = keep_ref.shape[1]
    row = lax.broadcasted_iota(jnp.int32, (count, count), 0)
    lane = lax.broadcasted_iota(jnp.int32, (count, count), 1)
    spread = jnp.where(row == lane, jnp.broadcast_to(keep_ref[...], (count, count)), 0)
    column = jnp.sum(spread.astype(jnp.float32), axis=1, keepdims=True)
    column_ref[...] = jnp.broadcast_to(column, column_ref.shape)

    def step(first, carry):
        for inner in range(8):
            index = first * 8 + inner
            rows_ref[pl.ds(index, 1), :] = residual_ref[pl.ds(slots_ref[0, index], 1), :]
        return carry

    lax.fori_loop(0, count // 8, step, 0)


def kept_part(region_keep, residual):
    count = region_keep.shape[1]
    vmem = pl.BlockSpec(memory_space=pltpu.VMEM)
    return pl.pallas_call(
        keep_kernel,
        out_shape=[jax.ShapeDtypeStruct((count, HEAD), jnp.float32)] * 2,
        in_specs=[pl.BlockSpec(memory_space=pltpu.SMEM), vmem, vmem],
        out_specs=[vmem, vmem],
        compiler_params=pltpu.CompilerParams(vmem_limit_bytes=8 * MIB),
        cost_estimate=pl.CostEstimate(flops=10**8, bytes_accessed=4 * MIB, transcendentals=0),
        name="kept_part",
    )(region_keep, region_keep, residual)


def chosen_kernel(got_ref, column_ref, rows_ref, chosen_ref, parts_ref, offs_ref):
    sources = got_ref.shape[0] // (CAP + 1)
    stride = CAP + 1
    column = column_ref[...]
    lane = lax.broadcasted_iota(jnp.int32, (1, LANES), 1)
    places = []
    for pair in range(sources // 2):
        first = 2 * pair * stride + CAP
        offs = jnp.where(lane < CAP, got_ref[first : first + 1], got_ref[first + stride : first + stride + 1])
        offs_ref[:, pair * LANES : (pair + 1) * LANES] = offs
        places.append(jnp.where(column == offs, 1.0, 0.0).astype(jnp.bfloat16))
    for source in range(sources):
        values = got_ref[source * stride : source * stride + CAP]
        high = values.astype(jnp.bfloat16)
        low = (values - high.astype(jnp.float32)).astype(jnp.bfloat16)
        parts_ref[source * CAP : (source + 1) * CAP, :HEAD] = high
        parts_ref[source * CAP : (source + 1) * CAP, HEAD:] = low
    summed = jnp.dot(jnp.concatenate(places, axis=1), parts_ref[...], preferred_element_type=jnp.float32)
    chosen_ref[...] = summed[:, :HEAD] + summed[:, HEAD:] + rows_ref[...]


def chosen_totals(got, column, rows):
    sources = got.shape[0] // (CAP + 1)
    vmem = pl.BlockSpec(memory_space=pltpu.VMEM)
    return pl.pallas_call(
        chosen_kernel,
        out_shape=[
            jax.ShapeDtypeStruct(rows.shape, jnp.float32),
            jax.ShapeDtypeStruct((sources * CAP, 2 * HEAD), jnp.bfloat16),
            jax.ShapeDtypeStruct((1, sources * CAP), jnp.float32),
        ],
        in_specs=[vmem] * 3,
        out_specs=[vmem] * 3,
        compiler_params=pltpu.CompilerParams(vmem_limit_bytes=16 * MIB),
        cost_estimate=pl.CostEstimate(flops=10**8, bytes_accessed=4 * MIB, transcendentals=0),
        name="chosen_totals",
    )(got, column, rows)


def refresh_kernel(length_ref, offs_ref, parts_ref, keep_ref, residual_ref, out_ref):
    rows = out_ref.shape[0]
    base = pl.program_id(0) * rows
    length = length_ref[0]
    parts = parts_ref[...]
    keep = keep_ref[...]
    for first in range(0, rows, SLOT_TILE):
        slot = lax.broadcasted_iota(jnp.int32, (SLOT_TILE, LANES), 0) + (base + first)
        slot_f = slot.astype(jnp.float32)
        place = jnp.concatenate(
            [
                jnp.where(slot_f == offs_ref[:, part : part + LANES], 1.0, 0.0).astype(jnp.bfloat16)
                for part in range(0, offs_ref.shape[1], LANES)
            ],
            axis=1,
        )
        summed = jnp.dot(place, parts, preferred_element_type=jnp.float32)
        hits = jnp.zeros((SLOT_TILE, LANES), jnp.float32)
        for part in range(0, keep.shape[1], LANES):
            hits = hits + jnp.where(slot == keep[:, part : part + LANES], 1.0, 0.0)
        named = jnp.sum(hits, axis=1, keepdims=True)
        survive = (slot < length) & (jnp.broadcast_to(named, slot.shape) == 0.0)
        totals = summed[:, :HEAD] + summed[:, HEAD:] + residual_ref[first : first + SLOT_TILE]
        out_ref[first : first + SLOT_TILE] = jnp.where(survive, totals, 0.0)


def refreshed_slots(length, offs, parts, region_keep, residual, steps):
    slots = residual.shape[0]
    rows = slots // steps
    whole = lambda shape: pl.BlockSpec(shape, lambda i: (0, 0))
    return pl.pallas_call(
        refresh_kernel,
        out_shape=jax.ShapeDtypeStruct((slots, HEAD), jnp.float32),
        grid=(steps,),
        in_specs=[
            pl.BlockSpec(memory_space=pltpu.SMEM),
            whole(offs.shape),
            whole(parts.shape),
            whole(region_keep.shape),
            pl.BlockSpec((rows, HEAD), lambda i: (i, 0)),
        ],
        out_specs=pl.BlockSpec((rows, HEAD), lambda i: (i, 0)),
        compiler_params=pltpu.CompilerParams(vmem_limit_bytes=24 * MIB),
        cost_estimate=pl.CostEstimate(flops=3 * 10**9, bytes_accessed=4 * MIB, transcendentals=0),
        name="refreshed_slots",
    )(length, offs, parts, region_keep, residual)


def body(activations, kv_grads, kept_blocks, region_bounds, region_keep, residual):
    inputs = activations[0, 0]
    grad_cols = kv_grads[0, 0]
    keep_count = kept_blocks.shape[3]
    residual = residual[0, 0]
    regions = lax.axis_size("rep")
    pods = lax.axis_size("outer")
    column_blocks = grad_cols.shape[1] // HEAD
    spanned = residual.shape[0] // column_blocks + 1
    band = -(-(spanned + LANES - 1) // LANES) * LANES
    owner = lax.axis_index("rep")
    length = (region_bounds[owner + 1] - region_bounds[owner]).reshape(1)

    sent = send_rows(region_bounds, kept_blocks.reshape(1, keep_count), inputs, grad_cols, band)
    got = lax.all_to_all(
        sent.reshape(regions, CAP + 1, 1, HEAD), "rep", split_axis=0, concat_axis=0, tiled=True
    ).reshape(regions * (CAP + 1), HEAD)
    column, rows = kept_part(region_keep, residual)
    chosen, parts, offs = chosen_totals(got, column, rows)
    share = chosen.shape[0] // pods
    shares = lax.all_to_all(
        chosen.reshape(pods, share, HEAD), "outer", split_axis=0, concat_axis=0, tiled=True
    )
    merged = jnp.sum(shares, axis=0)
    refreshed = refreshed_slots(length, offs, parts, region_keep, residual, 3)
    return (merged[None], refreshed[None, None])


def solution(mesh):
    placed = (
        P("outer", "rep", None, None),
        P("outer", "rep", None, "tp"),
        P("outer", "rep", "tp", None),
        P(),
        P("rep", None),
        P("outer", "rep", None, "tp"),
    )
    return jax.shard_map(
        body,
        mesh=mesh,
        in_specs=placed,
        out_specs=(P("rep", "outer", "tp"), P("outer", "rep", None, "tp")),
        check_vma=False,
    )
```

```python
import functools

import jax
import jax.numpy as jnp
from jax import lax
from jax.experimental import pallas as pl
from jax.experimental.pallas import tpu as pltpu
from jax.sharding import PartitionSpec as P

HEAD = 128
CAP = 64
LANES = 128
SLOT_TILE = 256
BATCH = 8
MIB = 1 << 20
CONTRACT_LAST = (((1,), (1,)), ((), ()))


def contract_last(left, right):
    return lax.dot_general(left, right, CONTRACT_LAST, preferred_element_type=jnp.float32)


def send_kernel(
    band, batch, bounds_hbm, ids_hbm, act_hbm, grad_hbm, out_hbm,
    bounds_ref, ids_ref, act_ref, grad_ref, out_ref, sems, out_sems,
):
    loads = [
        pltpu.make_async_copy(source, target, sems.at[place])
        for place, (source, target) in enumerate(
            ((bounds_hbm, bounds_ref), (ids_hbm, ids_ref), (act_hbm, act_ref), (grad_hbm, grad_ref))
        )
    ]
    for load in loads:
        load.start()
    loads[0].wait()
    loads[1].wait()
    regions = bounds_ref.shape[0] - 1
    keep_count = ids_ref.shape[1]
    width = act_ref.shape[1]
    column_blocks = grad_ref.shape[1] // HEAD
    column_bits = column_blocks.bit_length() - 1
    chunks = keep_count // LANES
    stride = CAP + 1

    region_row = lax.broadcasted_iota(jnp.int32, (regions, LANES), 0)
    starts = jnp.zeros((regions, LANES), jnp.int32)
    ends = jnp.zeros((regions, LANES), jnp.int32)
    for region in range(regions):
        starts = jnp.where(region_row == region, bounds_ref[region], starts)
        ends = jnp.where(region_row == region, bounds_ref[region + 1], ends)

    ids = [ids_ref[:, c * LANES : (c + 1) * LANES] for c in range(chunks)]
    owned = [(i >= starts) & (i < ends) for i in ids]
    owned_f = [jnp.where(o, 1.0, 0.0) for o in owned]
    stacked = jnp.concatenate(owned_f, axis=0).astype(jnp.bfloat16)
    before = lax.broadcasted_iota(jnp.int32, (LANES, 2 * LANES), 0)
    after = lax.broadcasted_iota(jnp.int32, (LANES, 2 * LANES), 1)
    ladder = jnp.where((before < after) | (after >= LANES), 1.0, 0.0).astype(jnp.bfloat16)
    counted = jnp.dot(stacked, ladder, preferred_element_type=jnp.float32)
    running = jnp.zeros((regions, LANES), jnp.float32)
    rank_row = lax.broadcasted_iota(jnp.int32, (2 * CAP, LANES), 0) & (CAP - 1)
    ranked, high_part, low_part = [], [], []
    for c in range(chunks):
        rows = slice(c * regions, (c + 1) * regions)
        here = counted[rows, :LANES] + running
        running = running + counted[rows, LANES:]
        rank = jnp.sum(owned_f[c] * here, axis=0, keepdims=True).astype(jnp.int32)
        ranked.append(jnp.where(rank_row == rank, 1.0, 0.0).astype(jnp.bfloat16))
        code = ids[c] + 1
        high_part.append((owned_f[c] * (code >> 8).astype(jnp.float32)).astype(jnp.bfloat16))
        low_part.append((owned_f[c] * (code & 255).astype(jnp.float32)).astype(jnp.bfloat16))
    ranked = jnp.concatenate(ranked, axis=1)
    high_part = jnp.concatenate(high_part, axis=1)
    low_part = jnp.concatenate(low_part, axis=1)
    by_region = 256.0 * contract_last(high_part, ranked) + contract_last(low_part, ranked) - 1.0
    ranked = ranked[:CAP]
    by_rank = 256.0 * contract_last(ranked, high_part) + contract_last(ranked, low_part) - 1.0
    offsets = jnp.where(by_region < 0.0, -1.0, by_region - starts.astype(jnp.float32))

    lane = lax.broadcasted_iota(jnp.int32, (CAP, LANES), 1)
    loads[2].wait()
    loads[3].wait()
    grads = grad_ref[...]
    stores = []
    for first in range(0, regions, batch):
        columns, picked = [], []
        for region in range(first, first + batch):
            wanted = jnp.broadcast_to(by_rank[:, region : region + 1], (CAP, LANES)).astype(jnp.int32)
            base = (bounds_ref[region] >> column_bits) & ~(LANES - 1)
            base = pl.multiple_of(jnp.minimum(base, width - band), LANES)
            place = (wanted >> column_bits) - base
            columns.append(wanted & (column_blocks - 1))
            chosen = jnp.concatenate(
                [
                    jnp.where(lane + part == place, 1.0, 0.0).astype(jnp.bfloat16)
                    for part in range(0, band, LANES)
                ],
                axis=1,
            )
            picked.append(contract_last(chosen, act_ref[:, pl.ds(base, band)]).astype(jnp.bfloat16))
        columns = jnp.concatenate(columns, axis=0)
        wide = jnp.dot(jnp.concatenate(picked, axis=0), grads, preferred_element_type=jnp.float32)
        block = wide[:, :HEAD]
        for column in range(1, column_blocks):
            block = jnp.where(columns == column, wide[:, column * HEAD : (column + 1) * HEAD], block)
        for step in range(batch):
            region = first + step
            out_ref[region * stride : region * stride + CAP, :] = block[step * CAP : (step + 1) * CAP]
            out_ref[region * stride + CAP : (region + 1) * stride, :] = offsets[region : region + 1]
        done = pl.ds(first * stride, batch * stride)
        store = pltpu.make_async_copy(out_ref.at[done], out_hbm.at[done], out_sems.at[first // batch])
        store.start()
        stores.append(store)
    for store in stores:
        store.wait()


def send_rows(region_bounds, block_ids, inputs, grad_cols, band):
    regions = region_bounds.shape[0] - 1
    hbm = pl.BlockSpec(memory_space=pltpu.HBM)
    rows = regions * (CAP + 1)
    return pl.pallas_call(
        functools.partial(send_kernel, band, BATCH),
        out_shape=jax.ShapeDtypeStruct((rows, HEAD), jnp.float32),
        in_specs=[hbm] * 4,
        out_specs=hbm,
        scratch_shapes=[
            pltpu.SMEM(region_bounds.shape, jnp.int32),
            pltpu.VMEM(block_ids.shape, jnp.int32),
            pltpu.VMEM(inputs.shape, inputs.dtype),
            pltpu.VMEM(grad_cols.shape, grad_cols.dtype),
            pltpu.VMEM((rows, HEAD), jnp.float32),
            pltpu.SemaphoreType.DMA((4,)),
            pltpu.SemaphoreType.DMA((regions // BATCH,)),
        ],
        compiler_params=pltpu.CompilerParams(vmem_limit_bytes=62 * MIB),
        cost_estimate=pl.CostEstimate(flops=10**9, bytes_accessed=4 * MIB, transcendentals=0),
        name="send_rows",
    )(region_bounds, block_ids, inputs, grad_cols)


def keep_kernel(slots_ref, keep_ref, residual_ref, column_ref, rows_ref):
    count = keep_ref.shape[1]
    row = lax.broadcasted_iota(jnp.int32, (count, count), 0)
    lane = lax.broadcasted_iota(jnp.int32, (count, count), 1)
    spread = jnp.where(row == lane, jnp.broadcast_to(keep_ref[...], (count, count)), 0)
    column = jnp.sum(spread.astype(jnp.float32), axis=1, keepdims=True)
    column_ref[...] = jnp.broadcast_to(column, column_ref.shape)

    def step(first, carry):
        for inner in range(8):
            index = first * 8 + inner
            rows_ref[pl.ds(index, 1), :] = residual_ref[pl.ds(slots_ref[0, index], 1), :]
        return carry

    lax.fori_loop(0, count // 8, step, 0)


def kept_part(region_keep, residual):
    count = region_keep.shape[1]
    vmem = pl.BlockSpec(memory_space=pltpu.VMEM)
    return pl.pallas_call(
        keep_kernel,
        out_shape=[jax.ShapeDtypeStruct((count, HEAD), jnp.float32)] * 2,
        in_specs=[pl.BlockSpec(memory_space=pltpu.SMEM), vmem, vmem],
        out_specs=[vmem, vmem],
        compiler_params=pltpu.CompilerParams(vmem_limit_bytes=8 * MIB),
        cost_estimate=pl.CostEstimate(flops=10**8, bytes_accessed=4 * MIB, transcendentals=0),
        name="kept_part",
    )(region_keep, region_keep, residual)


def split_rows(got_ref, parts_ref, offs_ref):
    stride = CAP + 1
    lane = lax.broadcasted_iota(jnp.int32, (1, LANES), 1)
    for pair in range(got_ref.shape[0] // stride // 2):
        first = 2 * pair * stride
        last = first + CAP
        offs_ref[:, pair * LANES : (pair + 1) * LANES] = jnp.where(
            lane < CAP, got_ref[last : last + 1], got_ref[last + stride : last + stride + 1]
        )
        for start, target in ((first, 2 * pair * CAP), (first + stride, (2 * pair + 1) * CAP)):
            values = got_ref[start : start + CAP]
            high = values.astype(jnp.bfloat16)
            low = (values - high.astype(jnp.float32)).astype(jnp.bfloat16)
            parts_ref[target : target + CAP, :HEAD] = high
            parts_ref[target : target + CAP, HEAD:] = low


def placed_sum(slots, offs_ref, parts_ref):
    place = jnp.concatenate(
        [
            jnp.where(slots == offs_ref[:, part : part + LANES], 1.0, 0.0).astype(jnp.bfloat16)
            for part in range(0, offs_ref.shape[1], LANES)
        ],
        axis=1,
    )
    summed = jnp.dot(place, parts_ref[...], preferred_element_type=jnp.float32)
    return summed[:, :HEAD] + summed[:, HEAD:]


def chosen_kernel(got_ref, column_ref, rows_ref, chosen_ref, parts_ref, offs_ref):
    split_rows(got_ref, parts_ref, offs_ref)
    chosen_ref[...] = placed_sum(column_ref[...], offs_ref, parts_ref) + rows_ref[...]


def part_scratch(got):
    filled = got.shape[0] // (CAP + 1) * CAP
    return [pltpu.VMEM((filled, 2 * HEAD), jnp.bfloat16), pltpu.VMEM((1, filled), jnp.float32)]


def chosen_totals(got, column, rows):
    vmem = pl.BlockSpec(memory_space=pltpu.VMEM)
    return pl.pallas_call(
        chosen_kernel,
        out_shape=jax.ShapeDtypeStruct(rows.shape, jnp.float32),
        in_specs=[vmem] * 3,
        out_specs=vmem,
        scratch_shapes=part_scratch(got),
        compiler_params=pltpu.CompilerParams(vmem_limit_bytes=16 * MIB),
        cost_estimate=pl.CostEstimate(flops=10**8, bytes_accessed=4 * MIB, transcendentals=0),
        name="chosen_totals",
    )(got, column, rows)


def refresh_kernel(length_ref, got_ref, keep_ref, residual_ref, out_ref, parts_ref, offs_ref):
    rows = out_ref.shape[0]
    base = pl.program_id(0) * rows
    length = length_ref[0]
    keep = keep_ref[...]

    @pl.when(base == 0)
    def _():
        split_rows(got_ref, parts_ref, offs_ref)

    for first in range(0, rows, SLOT_TILE):
        slot = lax.broadcasted_iota(jnp.int32, (SLOT_TILE, LANES), 0) + (base + first)
        hits = jnp.zeros((SLOT_TILE, LANES), jnp.float32)
        for part in range(0, keep.shape[1], LANES):
            hits = hits + jnp.where(slot == keep[:, part : part + LANES], 1.0, 0.0)
        named = jnp.sum(hits, axis=1, keepdims=True)
        survive = (slot < length) & (jnp.broadcast_to(named, slot.shape) == 0.0)
        summed = placed_sum(slot.astype(jnp.float32), offs_ref, parts_ref)
        totals = summed + residual_ref[first : first + SLOT_TILE]
        out_ref[first : first + SLOT_TILE] = jnp.where(survive, totals, 0.0)


def refreshed_slots(length, got, region_keep, residual, steps):
    slots = residual.shape[0]
    rows = slots // steps
    whole = lambda shape: pl.BlockSpec(shape, lambda i: (0, 0))
    return pl.pallas_call(
        refresh_kernel,
        out_shape=jax.ShapeDtypeStruct((slots, HEAD), jnp.float32),
        grid=(steps,),
        in_specs=[
            pl.BlockSpec(memory_space=pltpu.SMEM),
            pl.BlockSpec(memory_space=pltpu.VMEM),
            whole(region_keep.shape),
            pl.BlockSpec((rows, HEAD), lambda i: (i, 0)),
        ],
        out_specs=pl.BlockSpec((rows, HEAD), lambda i: (i, 0)),
        scratch_shapes=part_scratch(got),
        compiler_params=pltpu.CompilerParams(vmem_limit_bytes=24 * MIB),
        cost_estimate=pl.CostEstimate(flops=3 * 10**9, bytes_accessed=4 * MIB, transcendentals=0),
        name="refreshed_slots",
    )(length, got, region_keep, residual)


def body(activations, kv_grads, kept_blocks, region_bounds, region_keep, residual):
    inputs = activations[0, 0]
    grad_cols = kv_grads[0, 0]
    keep_count = kept_blocks.shape[3]
    residual = residual[0, 0]
    regions = lax.axis_size("rep")
    pods = lax.axis_size("outer")
    column_blocks = grad_cols.shape[1] // HEAD
    spanned = residual.shape[0] // column_blocks + 1
    band = -(-(spanned + LANES - 1) // LANES) * LANES
    owner = lax.axis_index("rep")
    length = (region_bounds[owner + 1] - region_bounds[owner]).reshape(1)

    sent = send_rows(region_bounds, kept_blocks.reshape(1, keep_count), inputs, grad_cols, band)
    got = lax.all_to_all(
        sent.reshape(regions, CAP + 1, 1, HEAD), "rep", split_axis=0, concat_axis=0, tiled=True
    ).reshape(regions * (CAP + 1), HEAD)
    column, rows = kept_part(region_keep, residual)
    chosen = chosen_totals(got, column, rows)
    share = chosen.shape[0] // pods
    shares = lax.all_to_all(
        chosen.reshape(pods, share, HEAD), "outer", split_axis=0, concat_axis=0, tiled=True
    )
    merged = jnp.sum(shares, axis=0)
    refreshed = refreshed_slots(length, got, region_keep, residual, 3)
    return (merged[None], refreshed[None, None])


def solution(mesh):
    placed = (
        P("outer", "rep", None, None),
        P("outer", "rep", None, "tp"),
        P("outer", "rep", "tp", None),
        P(),
        P("rep", None),
        P("outer", "rep", None, "tp"),
    )
    return jax.shard_map(
        body,
        mesh=mesh,
        in_specs=placed,
        out_specs=(P("rep", "outer", "tp"), P("outer", "rep", None, "tp")),
        check_vma=False,
    )
```

```python
import functools

import jax
import jax.numpy as jnp
from jax import lax
from jax.experimental import pallas as pl
from jax.experimental.pallas import tpu as pltpu
from jax.sharding import PartitionSpec as P

HEAD = 128
CAP = 64
LANES = 128
SLOT_TILE = 256
BATCH = 8
MIB = 1 << 20
CONTRACT_LAST = (((1,), (1,)), ((), ()))


def contract_last(left, right):
    return lax.dot_general(left, right, CONTRACT_LAST, preferred_element_type=jnp.float32)


def send_kernel(
    region_rows, band, batch, bounds_hbm, ids_hbm, act_hbm, grad_hbm, out_hbm,
    bounds_ref, ids_ref, act_ref, grad_ref, out_ref, sems, out_sems,
):
    half = act_ref.shape[1] // 2
    loads = [
        pltpu.make_async_copy(source, target, sems.at[place])
        for place, (source, target) in enumerate(
            (
                (bounds_hbm, bounds_ref),
                (ids_hbm, ids_ref),
                (act_hbm.at[:, pl.ds(0, half)], act_ref.at[:, pl.ds(0, half)]),
                (grad_hbm, grad_ref),
                (act_hbm.at[:, pl.ds(half, half)], act_ref.at[:, pl.ds(half, half)]),
            )
        )
    ]
    for load in loads:
        load.start()
    loads[0].wait()
    loads[1].wait()
    regions = bounds_ref.shape[0] - 1
    keep_count = ids_ref.shape[1]
    width = act_ref.shape[1]
    column_blocks = grad_ref.shape[1] // HEAD
    column_bits = column_blocks.bit_length() - 1
    chunks = keep_count // LANES
    stride = CAP + 1

    region_row = lax.broadcasted_iota(jnp.int32, (regions, LANES), 0)
    starts = jnp.zeros((regions, LANES), jnp.int32)
    ends = jnp.zeros((regions, LANES), jnp.int32)
    for region in range(regions):
        starts = jnp.where(region_row == region, bounds_ref[region], starts)
        ends = jnp.where(region_row == region, bounds_ref[region + 1], ends)

    ids = [ids_ref[:, c * LANES : (c + 1) * LANES] for c in range(chunks)]
    owned = [(i >= starts) & (i < ends) for i in ids]
    owned_f = [jnp.where(o, 1.0, 0.0) for o in owned]
    stacked = jnp.concatenate(owned_f, axis=0).astype(jnp.bfloat16)
    before = lax.broadcasted_iota(jnp.int32, (LANES, 2 * LANES), 0)
    after = lax.broadcasted_iota(jnp.int32, (LANES, 2 * LANES), 1)
    ladder = jnp.where((before < after) | (after >= LANES), 1.0, 0.0).astype(jnp.bfloat16)
    counted = jnp.dot(stacked, ladder, preferred_element_type=jnp.float32)
    running = jnp.zeros((regions, LANES), jnp.float32)
    rank_row = lax.broadcasted_iota(jnp.int32, (2 * CAP, LANES), 0) & (CAP - 1)
    ranked, high_part, low_part = [], [], []
    for c in range(chunks):
        rows = slice(c * regions, (c + 1) * regions)
        here = counted[rows, :LANES] + running
        running = running + counted[rows, LANES:]
        rank = jnp.sum(owned_f[c] * here, axis=0, keepdims=True).astype(jnp.int32)
        ranked.append(jnp.where(rank_row == rank, 1.0, 0.0).astype(jnp.bfloat16))
        code = ids[c] + 1
        high_part.append((owned_f[c] * (code >> 8).astype(jnp.float32)).astype(jnp.bfloat16))
        low_part.append((owned_f[c] * (code & 255).astype(jnp.float32)).astype(jnp.bfloat16))
    ranked = jnp.concatenate(ranked, axis=1)
    high_part = jnp.concatenate(high_part, axis=1)
    low_part = jnp.concatenate(low_part, axis=1)
    by_region = 256.0 * contract_last(high_part, ranked) + contract_last(low_part, ranked) - 1.0
    ranked = ranked[:CAP]
    by_rank = 256.0 * contract_last(ranked, high_part) + contract_last(ranked, low_part) - 1.0
    offsets = jnp.where(by_region < 0.0, -1.0, by_region - starts.astype(jnp.float32))

    lane = lax.broadcasted_iota(jnp.int32, (2 * CAP, LANES), 1)
    loads[3].wait()
    act_loads, waited = (loads[2], loads[4]), 0
    lane_low = lane.astype(jnp.bfloat16)
    paired = jnp.concatenate(
        [
            jnp.concatenate(
                [grad_ref[:, column * HEAD : (column + 1) * HEAD] for column in range(parity, column_blocks, 2)],
                axis=1,
            )
            for parity in range(2)
        ],
        axis=0,
    )
    stores = []
    for first in range(0, regions, batch):
        columns, picked = [], []
        reach = min(width, (first + batch) * region_rows + band)
        while waited < len(act_loads) and reach > waited * half:
            act_loads[waited].wait()
            waited += 1
        for region in range(first, first + batch, 2):
            wanted = jnp.concatenate(
                [jnp.broadcast_to(by_rank[:, r : r + 1], (CAP, LANES)) for r in (region, region + 1)], axis=0
            ).astype(jnp.int32)
            base = (bounds_ref[region] >> column_bits) & ~(LANES - 1)
            base = pl.multiple_of(jnp.minimum(base, width - band), LANES)
            place = (wanted >> column_bits) - base
            columns.append(wanted & (column_blocks - 1))
            low = (place & (LANES - 1)).astype(jnp.bfloat16)
            high = (place >> 7).astype(jnp.bfloat16)
            zero = jnp.zeros(low.shape, jnp.bfloat16)
            one = jnp.ones(low.shape, jnp.bfloat16)
            hot = jnp.where(low == lane_low, high, zero - 1)
            chosen = jnp.concatenate(
                [jnp.where(hot == part, one, zero) for part in range(band // LANES)], axis=1
            )
            picked.append(contract_last(chosen, act_ref[:, pl.ds(base, band)]).astype(jnp.bfloat16))
        columns = jnp.concatenate(columns, axis=0)
        rows = jnp.concatenate(picked, axis=0)
        odd = (columns & 1).astype(jnp.bfloat16)
        zero = jnp.zeros_like(rows)
        spread = jnp.concatenate([jnp.where(odd == 0, rows, zero), jnp.where(odd == 0, zero, rows)], axis=1)
        wide = jnp.dot(spread, paired, preferred_element_type=jnp.float32)
        pair = columns >> 1
        block = wide[:, :HEAD]
        for place in range(1, column_blocks // 2):
            block = jnp.where(pair == place, wide[:, place * HEAD : (place + 1) * HEAD], block)
        for step in range(batch):
            region = first + step
            out_ref[region * stride : region * stride + CAP, :] = block[step * CAP : (step + 1) * CAP]
            out_ref[region * stride + CAP : (region + 1) * stride, :] = offsets[region : region + 1]
        done = pl.ds(first * stride, batch * stride)
        store = pltpu.make_async_copy(out_ref.at[done], out_hbm.at[done], out_sems.at[first // batch])
        store.start()
        stores.append(store)
    for store in stores:
        store.wait()


def send_rows(region_bounds, block_ids, inputs, grad_cols, region_rows):
    regions = region_bounds.shape[0] - 1
    hbm = pl.BlockSpec(memory_space=pltpu.HBM)
    rows = regions * (CAP + 1)
    band = -(-(2 * region_rows + LANES) // (2 * LANES)) * (2 * LANES)
    return pl.pallas_call(
        functools.partial(send_kernel, region_rows, band, BATCH),
        out_shape=jax.ShapeDtypeStruct((rows, HEAD), jnp.float32),
        in_specs=[hbm] * 4,
        out_specs=hbm,
        scratch_shapes=[
            pltpu.SMEM(region_bounds.shape, jnp.int32),
            pltpu.VMEM(block_ids.shape, jnp.int32),
            pltpu.VMEM(inputs.shape, inputs.dtype),
            pltpu.VMEM(grad_cols.shape, grad_cols.dtype),
            pltpu.VMEM((rows, HEAD), jnp.float32),
            pltpu.SemaphoreType.DMA((5,)),
            pltpu.SemaphoreType.DMA((regions // BATCH,)),
        ],
        compiler_params=pltpu.CompilerParams(vmem_limit_bytes=62 * MIB),
        cost_estimate=pl.CostEstimate(flops=10**9, bytes_accessed=4 * MIB, transcendentals=0),
        name="send_rows",
    )(region_bounds, block_ids, inputs, grad_cols)


def keep_kernel(slots_ref, keep_ref, residual_ref, column_ref, rows_ref):
    count = keep_ref.shape[1]
    row = lax.broadcasted_iota(jnp.int32, (count, count), 0)
    lane = lax.broadcasted_iota(jnp.int32, (count, count), 1)
    spread = jnp.where(row == lane, jnp.broadcast_to(keep_ref[...], (count, count)), 0)
    column = jnp.sum(spread.astype(jnp.float32), axis=1, keepdims=True)
    column_ref[...] = jnp.broadcast_to(column, column_ref.shape)

    def step(first, carry):
        for inner in range(8):
            index = first * 8 + inner
            rows_ref[pl.ds(index, 1), :] = residual_ref[pl.ds(slots_ref[0, index], 1), :]
        return carry

    lax.fori_loop(0, count // 8, step, 0)


def kept_part(region_keep, residual):
    count = region_keep.shape[1]
    vmem = pl.BlockSpec(memory_space=pltpu.VMEM)
    return pl.pallas_call(
        keep_kernel,
        out_shape=[jax.ShapeDtypeStruct((count, HEAD), jnp.float32)] * 2,
        in_specs=[pl.BlockSpec(memory_space=pltpu.SMEM), vmem, vmem],
        out_specs=[vmem, vmem],
        compiler_params=pltpu.CompilerParams(vmem_limit_bytes=8 * MIB),
        cost_estimate=pl.CostEstimate(flops=10**8, bytes_accessed=4 * MIB, transcendentals=0),
        name="kept_part",
    )(region_keep, region_keep, residual)


def split_rows(got_ref, parts_ref, offs_ref):
    stride = CAP + 1
    lane = lax.broadcasted_iota(jnp.int32, (1, LANES), 1)
    for pair in range(got_ref.shape[0] // stride // 2):
        first = 2 * pair * stride
        last = first + CAP
        offs_ref[:, pair * LANES : (pair + 1) * LANES] = jnp.where(
            lane < CAP, got_ref[last : last + 1], got_ref[last + stride : last + stride + 1]
        )
        for start, target in ((first, 2 * pair * CAP), (first + stride, (2 * pair + 1) * CAP)):
            values = got_ref[start : start + CAP]
            high = values.astype(jnp.bfloat16)
            low = (values - high.astype(jnp.float32)).astype(jnp.bfloat16)
            parts_ref[target : target + CAP, :HEAD] = high
            parts_ref[target : target + CAP, HEAD:] = low


def placed_sum(slots, offs_ref, parts_ref):
    place = jnp.concatenate(
        [
            jnp.where(slots == offs_ref[:, part : part + LANES], 1.0, 0.0).astype(jnp.bfloat16)
            for part in range(0, offs_ref.shape[1], LANES)
        ],
        axis=1,
    )
    summed = jnp.dot(place, parts_ref[...], preferred_element_type=jnp.float32)
    return summed[:, :HEAD] + summed[:, HEAD:]


def chosen_kernel(got_ref, column_ref, rows_ref, chosen_ref, parts_ref, offs_ref):
    split_rows(got_ref, parts_ref, offs_ref)
    chosen_ref[...] = placed_sum(column_ref[...], offs_ref, parts_ref) + rows_ref[...]


def part_scratch(got):
    filled = got.shape[0] // (CAP + 1) * CAP
    return [pltpu.VMEM((filled, 2 * HEAD), jnp.bfloat16), pltpu.VMEM((1, filled), jnp.float32)]


def chosen_totals(got, column, rows):
    vmem = pl.BlockSpec(memory_space=pltpu.VMEM)
    return pl.pallas_call(
        chosen_kernel,
        out_shape=jax.ShapeDtypeStruct(rows.shape, jnp.float32),
        in_specs=[vmem] * 3,
        out_specs=vmem,
        scratch_shapes=part_scratch(got),
        compiler_params=pltpu.CompilerParams(vmem_limit_bytes=16 * MIB),
        cost_estimate=pl.CostEstimate(flops=10**8, bytes_accessed=4 * MIB, transcendentals=0),
        name="chosen_totals",
    )(got, column, rows)


def refresh_kernel(length_ref, got_ref, keep_ref, residual_ref, out_ref, parts_ref, offs_ref):
    rows = out_ref.shape[0]
    base = pl.program_id(0) * rows
    length = length_ref[0]
    keep = keep_ref[...]

    @pl.when(base == 0)
    def _():
        split_rows(got_ref, parts_ref, offs_ref)

    for first in range(0, rows, SLOT_TILE):
        slot = lax.broadcasted_iota(jnp.int32, (SLOT_TILE, LANES), 0) + (base + first)
        hits = jnp.zeros((SLOT_TILE, LANES), jnp.float32)
        for part in range(0, keep.shape[1], LANES):
            hits = hits + jnp.where(slot == keep[:, part : part + LANES], 1.0, 0.0)
        named = jnp.sum(hits, axis=1, keepdims=True)
        survive = (slot < length) & (jnp.broadcast_to(named, slot.shape) == 0.0)
        summed = placed_sum(slot.astype(jnp.float32), offs_ref, parts_ref)
        totals = summed + residual_ref[first : first + SLOT_TILE]
        out_ref[first : first + SLOT_TILE] = jnp.where(survive, totals, 0.0)


def refreshed_slots(length, got, region_keep, residual, steps):
    slots = residual.shape[0]
    rows = slots // steps
    whole = lambda shape: pl.BlockSpec(shape, lambda i: (0, 0))
    return pl.pallas_call(
        refresh_kernel,
        out_shape=jax.ShapeDtypeStruct((slots, HEAD), jnp.float32),
        grid=(steps,),
        in_specs=[
            pl.BlockSpec(memory_space=pltpu.SMEM),
            pl.BlockSpec(memory_space=pltpu.VMEM),
            whole(region_keep.shape),
            pl.BlockSpec((rows, HEAD), lambda i: (i, 0)),
        ],
        out_specs=pl.BlockSpec((rows, HEAD), lambda i: (i, 0)),
        scratch_shapes=part_scratch(got),
        compiler_params=pltpu.CompilerParams(vmem_limit_bytes=24 * MIB),
        cost_estimate=pl.CostEstimate(flops=3 * 10**9, bytes_accessed=4 * MIB, transcendentals=0),
        name="refreshed_slots",
    )(length, got, region_keep, residual)


def body(activations, kv_grads, kept_blocks, region_bounds, region_keep, residual):
    inputs = activations[0, 0]
    grad_cols = kv_grads[0, 0]
    keep_count = kept_blocks.shape[3]
    residual = residual[0, 0]
    regions = lax.axis_size("rep")
    pods = lax.axis_size("outer")
    column_blocks = grad_cols.shape[1] // HEAD
    region_rows = residual.shape[0] // column_blocks
    owner = lax.axis_index("rep")
    length = (region_bounds[owner + 1] - region_bounds[owner]).reshape(1)

    sent = send_rows(region_bounds, kept_blocks.reshape(1, keep_count), inputs, grad_cols, region_rows)
    got = lax.all_to_all(
        sent.reshape(regions, CAP + 1, 1, HEAD), "rep", split_axis=0, concat_axis=0, tiled=True
    ).reshape(regions * (CAP + 1), HEAD)
    column, rows = kept_part(region_keep, residual)
    chosen = chosen_totals(got, column, rows)
    share = chosen.shape[0] // pods
    shares = lax.all_to_all(
        chosen.reshape(pods, share, HEAD), "outer", split_axis=0, concat_axis=0, tiled=True
    )
    merged = jnp.sum(shares, axis=0)
    refreshed = refreshed_slots(length, got, region_keep, residual, 3)
    return (merged[None], refreshed[None, None])


def solution(mesh):
    placed = (
        P("outer", "rep", None, None),
        P("outer", "rep", None, "tp"),
        P("outer", "rep", "tp", None),
        P(),
        P("rep", None),
        P("outer", "rep", None, "tp"),
    )
    return jax.shard_map(
        body,
        mesh=mesh,
        in_specs=placed,
        out_specs=(P("rep", "outer", "tp"), P("outer", "rep", None, "tp")),
        check_vma=False,
    )
```

```python
import functools

import jax
import jax.numpy as jnp
from jax import lax
from jax.experimental import pallas as pl
from jax.experimental.pallas import tpu as pltpu
from jax.sharding import PartitionSpec as P

HEAD = 128
CAP = 64
LANES = 128
SLOT_TILE = 256
BATCH = 8
MIB = 1 << 20
CONTRACT_LAST = (((1,), (1,)), ((), ()))


def contract_last(left, right):
    return lax.dot_general(left, right, CONTRACT_LAST, preferred_element_type=jnp.float32)


def seating(regions):
    return [regions - 1 - seat for seat in range(regions)]


def send_kernel(
    region_rows, band, batch, bounds_hbm, ids_hbm, act_hbm, grad_hbm, out_hbm,
    bounds_ref, ids_ref, act_ref, grad_ref, out_ref, sems, out_sems,
):
    half = act_ref.shape[1] // 2
    loads = [
        pltpu.make_async_copy(source, target, sems.at[place])
        for place, (source, target) in enumerate(
            (
                (bounds_hbm, bounds_ref),
                (ids_hbm, ids_ref),
                (act_hbm.at[:, pl.ds(0, half)], act_ref.at[:, pl.ds(0, half)]),
                (grad_hbm, grad_ref),
                (act_hbm.at[:, pl.ds(half, half)], act_ref.at[:, pl.ds(half, half)]),
            )
        )
    ]
    for load in loads:
        load.start()
    loads[0].wait()
    loads[1].wait()
    regions = bounds_ref.shape[0] - 1
    keep_count = ids_ref.shape[1]
    width = act_ref.shape[1]
    column_blocks = grad_ref.shape[1] // HEAD
    column_bits = column_blocks.bit_length() - 1
    seats = seating(regions)
    chunks = keep_count // LANES
    stride = CAP + 1

    region_row = lax.broadcasted_iota(jnp.int32, (regions, LANES), 0)
    starts = jnp.zeros((regions, LANES), jnp.int32)
    ends = jnp.zeros((regions, LANES), jnp.int32)
    for region in range(regions):
        starts = jnp.where(region_row == region, bounds_ref[region], starts)
        ends = jnp.where(region_row == region, bounds_ref[region + 1], ends)

    ids = [ids_ref[:, c * LANES : (c + 1) * LANES] for c in range(chunks)]
    owned = [(i >= starts) & (i < ends) for i in ids]
    owned_f = [jnp.where(o, 1.0, 0.0) for o in owned]
    stacked = jnp.concatenate(owned_f, axis=0).astype(jnp.bfloat16)
    before = lax.broadcasted_iota(jnp.int32, (LANES, 2 * LANES), 0)
    after = lax.broadcasted_iota(jnp.int32, (LANES, 2 * LANES), 1)
    ladder = jnp.where((before < after) | (after >= LANES), 1.0, 0.0).astype(jnp.bfloat16)
    counted = jnp.dot(stacked, ladder, preferred_element_type=jnp.float32)
    running = jnp.zeros((regions, LANES), jnp.float32)
    rank_row = lax.broadcasted_iota(jnp.int32, (2 * CAP, LANES), 0) & (CAP - 1)
    ranked, high_part, low_part = [], [], []
    for c in range(chunks):
        rows = slice(c * regions, (c + 1) * regions)
        here = counted[rows, :LANES] + running
        running = running + counted[rows, LANES:]
        rank = jnp.sum(owned_f[c] * here, axis=0, keepdims=True).astype(jnp.int32)
        ranked.append(jnp.where(rank_row == rank, 1.0, 0.0).astype(jnp.bfloat16))
        code = ids[c] + 1
        high_part.append((owned_f[c] * (code >> 8).astype(jnp.float32)).astype(jnp.bfloat16))
        low_part.append((owned_f[c] * (code & 255).astype(jnp.float32)).astype(jnp.bfloat16))
    ranked = jnp.concatenate(ranked, axis=1)
    high_part = jnp.concatenate(high_part, axis=1)
    low_part = jnp.concatenate(low_part, axis=1)
    by_region = 256.0 * contract_last(high_part, ranked) + contract_last(low_part, ranked) - 1.0
    ranked = ranked[:CAP]
    by_rank = 256.0 * contract_last(ranked, high_part) + contract_last(ranked, low_part) - 1.0
    offsets = jnp.where(by_region < 0.0, -1.0, by_region - starts.astype(jnp.float32))

    lane = lax.broadcasted_iota(jnp.int32, (2 * CAP, LANES), 1)
    loads[3].wait()
    act_loads, waited = (loads[2], loads[4]), 0
    lane_low = lane.astype(jnp.bfloat16)
    paired = jnp.concatenate(
        [
            jnp.concatenate(
                [grad_ref[:, column * HEAD : (column + 1) * HEAD] for column in range(parity, column_blocks, 2)],
                axis=1,
            )
            for parity in range(2)
        ],
        axis=0,
    )
    held = []
    for first in range(0, regions, batch):
        columns, picked = [], []
        reach = min(width, (first + batch) * region_rows + band)
        while waited < len(act_loads) and reach > waited * half:
            act_loads[waited].wait()
            waited += 1
        for region in range(first, first + batch, 2):
            wanted = jnp.concatenate(
                [jnp.broadcast_to(by_rank[:, r : r + 1], (CAP, LANES)) for r in (region, region + 1)], axis=0
            ).astype(jnp.int32)
            base = (bounds_ref[region] >> column_bits) & ~(LANES - 1)
            base = pl.multiple_of(jnp.minimum(base, width - band), LANES)
            place = (wanted >> column_bits) - base
            columns.append(wanted & (column_blocks - 1))
            low = (place & (LANES - 1)).astype(jnp.bfloat16)
            high = (place >> 7).astype(jnp.bfloat16)
            zero = jnp.zeros(low.shape, jnp.bfloat16)
            one = jnp.ones(low.shape, jnp.bfloat16)
            hot = jnp.where(low == lane_low, high, zero - 1)
            chosen = jnp.concatenate(
                [jnp.where(hot == part, one, zero) for part in range(band // LANES)], axis=1
            )
            picked.append(contract_last(chosen, act_ref[:, pl.ds(base, band)]).astype(jnp.bfloat16))
        held.append((first, jnp.concatenate(columns, axis=0), jnp.concatenate(picked, axis=0)))

    stores = []
    for first, columns, rows in held:
        odd = (columns & 1).astype(jnp.bfloat16)
        zero = jnp.zeros_like(rows)
        spread = jnp.concatenate([jnp.where(odd == 0, rows, zero), jnp.where(odd == 0, zero, rows)], axis=1)
        wide = jnp.dot(spread, paired, preferred_element_type=jnp.float32)
        pair = columns >> 1
        block = wide[:, :HEAD]
        for place in range(1, column_blocks // 2):
            block = jnp.where(pair == place, wide[:, place * HEAD : (place + 1) * HEAD], block)
        for step in range(batch):
            region = first + step
            seat = seats.index(region)
            out_ref[seat * stride : seat * stride + CAP, :] = block[step * CAP : (step + 1) * CAP]
            out_ref[seat * stride + CAP : (seat + 1) * stride, :] = offsets[region : region + 1]
        block_first = min(seats.index(region) for region in range(first, first + batch))
        done = pl.ds(block_first * stride, batch * stride)
        store = pltpu.make_async_copy(out_ref.at[done], out_hbm.at[done], out_sems.at[first // batch])
        store.start()
        stores.append(store)
    for store in stores:
        store.wait()


def send_rows(region_bounds, block_ids, inputs, grad_cols, region_rows):
    regions = region_bounds.shape[0] - 1
    hbm = pl.BlockSpec(memory_space=pltpu.HBM)
    rows = regions * (CAP + 1)
    band = -(-(2 * region_rows + LANES) // (2 * LANES)) * (2 * LANES)
    return pl.pallas_call(
        functools.partial(send_kernel, region_rows, band, BATCH),
        out_shape=jax.ShapeDtypeStruct((rows, HEAD), jnp.float32),
        in_specs=[hbm] * 4,
        out_specs=hbm,
        scratch_shapes=[
            pltpu.SMEM(region_bounds.shape, jnp.int32),
            pltpu.VMEM(block_ids.shape, jnp.int32),
            pltpu.VMEM(inputs.shape, inputs.dtype),
            pltpu.VMEM(grad_cols.shape, grad_cols.dtype),
            pltpu.VMEM((rows, HEAD), jnp.float32),
            pltpu.SemaphoreType.DMA((5,)),
            pltpu.SemaphoreType.DMA((regions // BATCH,)),
        ],
        compiler_params=pltpu.CompilerParams(vmem_limit_bytes=62 * MIB),
        cost_estimate=pl.CostEstimate(flops=10**9, bytes_accessed=4 * MIB, transcendentals=0),
        name="send_rows",
    )(region_bounds, block_ids, inputs, grad_cols)


def keep_kernel(slots_ref, keep_ref, residual_ref, column_ref, rows_ref):
    count = keep_ref.shape[1]
    row = lax.broadcasted_iota(jnp.int32, (count, count), 0)
    lane = lax.broadcasted_iota(jnp.int32, (count, count), 1)
    spread = jnp.where(row == lane, jnp.broadcast_to(keep_ref[...], (count, count)), 0)
    column = jnp.sum(spread.astype(jnp.float32), axis=1, keepdims=True)
    column_ref[...] = jnp.broadcast_to(column, column_ref.shape)

    def step(first, carry):
        for inner in range(8):
            index = first * 8 + inner
            rows_ref[pl.ds(index, 1), :] = residual_ref[pl.ds(slots_ref[0, index], 1), :]
        return carry

    lax.fori_loop(0, count // 8, step, 0)


def kept_part(region_keep, residual):
    count = region_keep.shape[1]
    vmem = pl.BlockSpec(memory_space=pltpu.VMEM)
    return pl.pallas_call(
        keep_kernel,
        out_shape=[jax.ShapeDtypeStruct((count, HEAD), jnp.float32)] * 2,
        in_specs=[pl.BlockSpec(memory_space=pltpu.SMEM), vmem, vmem],
        out_specs=[vmem, vmem],
        compiler_params=pltpu.CompilerParams(vmem_limit_bytes=8 * MIB),
        cost_estimate=pl.CostEstimate(flops=10**8, bytes_accessed=4 * MIB, transcendentals=0),
        name="kept_part",
    )(region_keep, region_keep, residual)


def split_rows(got_ref, parts_ref, offs_ref):
    stride = CAP + 1
    lane = lax.broadcasted_iota(jnp.int32, (1, LANES), 1)
    for pair in range(got_ref.shape[0] // stride // 2):
        first = 2 * pair * stride
        last = first + CAP
        offs_ref[:, pair * LANES : (pair + 1) * LANES] = jnp.where(
            lane < CAP, got_ref[last : last + 1], got_ref[last + stride : last + stride + 1]
        )
        for start, target in ((first, 2 * pair * CAP), (first + stride, (2 * pair + 1) * CAP)):
            values = got_ref[start : start + CAP]
            high = values.astype(jnp.bfloat16)
            low = (values - high.astype(jnp.float32)).astype(jnp.bfloat16)
            parts_ref[target : target + CAP, :HEAD] = high
            parts_ref[target : target + CAP, HEAD:] = low


def placed_sum(slots, offs_ref, parts_ref):
    place = jnp.concatenate(
        [
            jnp.where(slots == offs_ref[:, part : part + LANES], 1.0, 0.0).astype(jnp.bfloat16)
            for part in range(0, offs_ref.shape[1], LANES)
        ],
        axis=1,
    )
    summed = jnp.dot(place, parts_ref[...], preferred_element_type=jnp.float32)
    return summed[:, :HEAD] + summed[:, HEAD:]


def chosen_kernel(got_ref, column_ref, rows_ref, chosen_ref, parts_ref, offs_ref):
    split_rows(got_ref, parts_ref, offs_ref)
    chosen_ref[...] = placed_sum(column_ref[...], offs_ref, parts_ref) + rows_ref[...]


def part_scratch(got):
    filled = got.shape[0] // (CAP + 1) * CAP
    return [pltpu.VMEM((filled, 2 * HEAD), jnp.bfloat16), pltpu.VMEM((1, filled), jnp.float32)]


def chosen_totals(got, column, rows):
    vmem = pl.BlockSpec(memory_space=pltpu.VMEM)
    return pl.pallas_call(
        chosen_kernel,
        out_shape=jax.ShapeDtypeStruct(rows.shape, jnp.float32),
        in_specs=[vmem] * 3,
        out_specs=vmem,
        scratch_shapes=part_scratch(got),
        compiler_params=pltpu.CompilerParams(vmem_limit_bytes=16 * MIB),
        cost_estimate=pl.CostEstimate(flops=10**8, bytes_accessed=4 * MIB, transcendentals=0),
        name="chosen_totals",
    )(got, column, rows)


def refresh_kernel(length_ref, got_ref, keep_ref, residual_ref, out_ref, parts_ref, offs_ref):
    rows = out_ref.shape[0]
    base = pl.program_id(0) * rows
    length = length_ref[0]
    keep = keep_ref[...]

    @pl.when(base == 0)
    def _():
        split_rows(got_ref, parts_ref, offs_ref)

    for first in range(0, rows, SLOT_TILE):
        slot = lax.broadcasted_iota(jnp.int32, (SLOT_TILE, LANES), 0) + (base + first)
        hits = jnp.zeros((SLOT_TILE, LANES), jnp.float32)
        for part in range(0, keep.shape[1], LANES):
            hits = hits + jnp.where(slot == keep[:, part : part + LANES], 1.0, 0.0)
        named = jnp.sum(hits, axis=1, keepdims=True)
        survive = (slot < length) & (jnp.broadcast_to(named, slot.shape) == 0.0)
        summed = placed_sum(slot.astype(jnp.float32), offs_ref, parts_ref)
        totals = summed + residual_ref[first : first + SLOT_TILE]
        out_ref[first : first + SLOT_TILE] = jnp.where(survive, totals, 0.0)


def refreshed_slots(length, got, region_keep, residual, steps):
    slots = residual.shape[0]
    rows = slots // steps
    whole = lambda shape: pl.BlockSpec(shape, lambda i: (0, 0))
    return pl.pallas_call(
        refresh_kernel,
        out_shape=jax.ShapeDtypeStruct((slots, HEAD), jnp.float32),
        grid=(steps,),
        in_specs=[
            pl.BlockSpec(memory_space=pltpu.SMEM),
            pl.BlockSpec(memory_space=pltpu.VMEM),
            whole(region_keep.shape),
            pl.BlockSpec((rows, HEAD), lambda i: (i, 0)),
        ],
        out_specs=pl.BlockSpec((rows, HEAD), lambda i: (i, 0)),
        scratch_shapes=part_scratch(got),
        compiler_params=pltpu.CompilerParams(vmem_limit_bytes=24 * MIB),
        cost_estimate=pl.CostEstimate(flops=3 * 10**9, bytes_accessed=4 * MIB, transcendentals=0),
        name="refreshed_slots",
    )(length, got, region_keep, residual)


def body(activations, kv_grads, kept_blocks, region_bounds, region_keep, residual):
    inputs = activations[0, 0]
    grad_cols = kv_grads[0, 0]
    keep_count = kept_blocks.shape[3]
    residual = residual[0, 0]
    regions = lax.axis_size("rep")
    pods = lax.axis_size("outer")
    column_blocks = grad_cols.shape[1] // HEAD
    region_rows = residual.shape[0] // column_blocks
    owner = lax.axis_index("rep")
    length = (region_bounds[owner + 1] - region_bounds[owner]).reshape(1)

    sent = send_rows(region_bounds, kept_blocks.reshape(1, keep_count), inputs, grad_cols, region_rows)
    got = lax.all_to_all(
        sent.reshape(regions, CAP + 1, 1, HEAD),
        "rep",
        split_axis=0,
        concat_axis=0,
        tiled=True,
        axis_index_groups=[seating(regions)],
    ).reshape(regions * (CAP + 1), HEAD)
    column, rows = kept_part(region_keep, residual)
    chosen = chosen_totals(got, column, rows)
    share = chosen.shape[0] // pods
    shares = lax.all_to_all(
        chosen.reshape(pods, share, HEAD), "outer", split_axis=0, concat_axis=0, tiled=True
    )
    merged = jnp.sum(shares, axis=0)
    refreshed = refreshed_slots(length, got, region_keep, residual, 3)
    return (merged[None], refreshed[None, None])


def solution(mesh):
    placed = (
        P("outer", "rep", None, None),
        P("outer", "rep", None, "tp"),
        P("outer", "rep", "tp", None),
        P(),
        P("rep", None),
        P("outer", "rep", None, "tp"),
    )
    return jax.shard_map(
        body,
        mesh=mesh,
        in_specs=placed,
        out_specs=(P("rep", "outer", "tp"), P("outer", "rep", None, "tp")),
        check_vma=False,
    )
```

```python
import functools

import jax
import jax.numpy as jnp
from jax import lax
from jax.experimental import pallas as pl
from jax.experimental.pallas import tpu as pltpu
from jax.sharding import PartitionSpec as P

HEAD = 128
CAP = 64
LANES = 128
SLOT_TILE = 256
BATCH = 8
MIB = 1 << 20
CONTRACT_LAST = (((1,), (1,)), ((), ()))


def contract_last(left, right):
    return lax.dot_general(left, right, CONTRACT_LAST, preferred_element_type=jnp.float32)


def seating(regions):
    return [regions - 1 - seat for seat in range(regions)]


def send_kernel(
    region_rows, band, batch, bounds_hbm, ids_hbm, act_hbm, grad_hbm, out_hbm,
    bounds_ref, ids_ref, act_ref, grad_ref, out_ref, sems, out_sems,
):
    half = act_ref.shape[1] // 2
    loads = [
        pltpu.make_async_copy(source, target, sems.at[place])
        for place, (source, target) in enumerate(
            (
                (bounds_hbm, bounds_ref),
                (ids_hbm, ids_ref),
                (act_hbm.at[:, pl.ds(0, half)], act_ref.at[:, pl.ds(0, half)]),
                (grad_hbm, grad_ref),
                (act_hbm.at[:, pl.ds(half, half)], act_ref.at[:, pl.ds(half, half)]),
            )
        )
    ]
    for load in loads:
        load.start()
    loads[0].wait()
    loads[1].wait()
    regions = bounds_ref.shape[0] - 1
    keep_count = ids_ref.shape[1]
    width = act_ref.shape[1]
    column_blocks = grad_ref.shape[1] // HEAD
    column_bits = column_blocks.bit_length() - 1
    seats = seating(regions)
    chunks = keep_count // LANES
    stride = CAP + 1

    region_row = lax.broadcasted_iota(jnp.int32, (regions, LANES), 0)
    starts = jnp.zeros((regions, LANES), jnp.int32)
    ends = jnp.zeros((regions, LANES), jnp.int32)
    for region in range(regions):
        starts = jnp.where(region_row == region, bounds_ref[region], starts)
        ends = jnp.where(region_row == region, bounds_ref[region + 1], ends)

    ids = [ids_ref[:, c * LANES : (c + 1) * LANES] for c in range(chunks)]
    owned = [(i >= starts) & (i < ends) for i in ids]
    owned_f = [jnp.where(o, 1.0, 0.0) for o in owned]
    stacked = jnp.concatenate(owned_f, axis=0).astype(jnp.bfloat16)
    before = lax.broadcasted_iota(jnp.int32, (LANES, 2 * LANES), 0)
    after = lax.broadcasted_iota(jnp.int32, (LANES, 2 * LANES), 1)
    ladder = jnp.where((before < after) | (after >= LANES), 1.0, 0.0).astype(jnp.bfloat16)
    counted = jnp.dot(stacked, ladder, preferred_element_type=jnp.float32)
    running = jnp.zeros((regions, LANES), jnp.float32)
    rank_row = lax.broadcasted_iota(jnp.int32, (2 * CAP, LANES), 0) & (CAP - 1)
    ranked, high_part, low_part = [], [], []
    for c in range(chunks):
        rows = slice(c * regions, (c + 1) * regions)
        here = counted[rows, :LANES] + running
        running = running + counted[rows, LANES:]
        rank = jnp.sum(owned_f[c] * here, axis=0, keepdims=True).astype(jnp.int32)
        ranked.append(jnp.where(rank_row == rank, 1.0, 0.0).astype(jnp.bfloat16))
        code = ids[c] + 1
        high_part.append((owned_f[c] * (code >> 8).astype(jnp.float32)).astype(jnp.bfloat16))
        low_part.append((owned_f[c] * (code & 255).astype(jnp.float32)).astype(jnp.bfloat16))
    ranked = jnp.concatenate(ranked, axis=1)
    high_part = jnp.concatenate(high_part, axis=1)
    low_part = jnp.concatenate(low_part, axis=1)
    by_region = 256.0 * contract_last(high_part, ranked) + contract_last(low_part, ranked) - 1.0
    ranked = ranked[:CAP]
    by_rank = 256.0 * contract_last(ranked, high_part) + contract_last(ranked, low_part) - 1.0
    offsets = jnp.where(by_region < 0.0, -1.0, by_region - starts.astype(jnp.float32))

    lane = lax.broadcasted_iota(jnp.int32, (2 * CAP, LANES), 1)
    loads[3].wait()
    act_loads, waited = (loads[2], loads[4]), 0
    lane_low = lane.astype(jnp.bfloat16)
    paired = jnp.concatenate(
        [
            jnp.concatenate(
                [grad_ref[:, column * HEAD : (column + 1) * HEAD] for column in range(parity, column_blocks, 2)],
                axis=1,
            )
            for parity in range(2)
        ],
        axis=0,
    )
    held = []
    for first in range(0, regions, batch):
        columns, picked = [], []
        reach = min(width, (first + batch) * region_rows + band)
        while waited < len(act_loads) and reach > waited * half:
            act_loads[waited].wait()
            waited += 1
        for region in range(first, first + batch, 2):
            wanted = jnp.concatenate(
                [jnp.broadcast_to(by_rank[:, r : r + 1], (CAP, LANES)) for r in (region, region + 1)], axis=0
            ).astype(jnp.int32)
            base = (bounds_ref[region] >> column_bits) & ~(LANES - 1)
            base = pl.multiple_of(jnp.minimum(base, width - band), LANES)
            place = (wanted >> column_bits) - base
            columns.append(wanted & (column_blocks - 1))
            low = (place & (LANES - 1)).astype(jnp.bfloat16)
            high = (place >> 7).astype(jnp.bfloat16)
            zero = jnp.zeros(low.shape, jnp.bfloat16)
            one = jnp.ones(low.shape, jnp.bfloat16)
            hot = jnp.where(low == lane_low, high, zero - 1)
            chosen = jnp.concatenate(
                [jnp.where(hot == part, one, zero) for part in range(band // LANES)], axis=1
            )
            picked.append(contract_last(chosen, act_ref[:, pl.ds(base, band)]).astype(jnp.bfloat16))
        held.append((first, jnp.concatenate(columns, axis=0), jnp.concatenate(picked, axis=0)))

    stores = []
    for first, columns, rows in held:
        odd = (columns & 1).astype(jnp.bfloat16)
        zero = jnp.zeros_like(rows)
        spread = jnp.concatenate([jnp.where(odd == 0, rows, zero), jnp.where(odd == 0, zero, rows)], axis=1)
        wide = jnp.dot(spread, paired, preferred_element_type=jnp.float32)
        pair = columns >> 1
        block = wide[:, :HEAD]
        for place in range(1, column_blocks // 2):
            block = jnp.where(pair == place, wide[:, place * HEAD : (place + 1) * HEAD], block)
        for step in range(batch):
            region = first + step
            seat = seats.index(region)
            out_ref[seat * stride : seat * stride + CAP, :] = block[step * CAP : (step + 1) * CAP]
            out_ref[seat * stride + CAP : (seat + 1) * stride, :] = offsets[region : region + 1]
        block_first = min(seats.index(region) for region in range(first, first + batch))
        done = pl.ds(block_first * stride, batch * stride)
        store = pltpu.make_async_copy(out_ref.at[done], out_hbm.at[done], out_sems.at[first // batch])
        store.start()
        stores.append(store)
    for store in stores:
        store.wait()


def send_rows(region_bounds, block_ids, inputs, grad_cols, region_rows):
    regions = region_bounds.shape[0] - 1
    hbm = pl.BlockSpec(memory_space=pltpu.HBM)
    rows = regions * (CAP + 1)
    band = -(-(2 * region_rows + LANES) // (2 * LANES)) * (2 * LANES)
    return pl.pallas_call(
        functools.partial(send_kernel, region_rows, band, BATCH),
        out_shape=jax.ShapeDtypeStruct((rows, HEAD), jnp.float32),
        in_specs=[hbm] * 4,
        out_specs=hbm,
        scratch_shapes=[
            pltpu.SMEM(region_bounds.shape, jnp.int32),
            pltpu.VMEM(block_ids.shape, jnp.int32),
            pltpu.VMEM(inputs.shape, inputs.dtype),
            pltpu.VMEM(grad_cols.shape, grad_cols.dtype),
            pltpu.VMEM((rows, HEAD), jnp.float32),
            pltpu.SemaphoreType.DMA((5,)),
            pltpu.SemaphoreType.DMA((regions // BATCH,)),
        ],
        compiler_params=pltpu.CompilerParams(vmem_limit_bytes=62 * MIB),
        cost_estimate=pl.CostEstimate(flops=10**9, bytes_accessed=4 * MIB, transcendentals=0),
        name="send_rows",
    )(region_bounds, block_ids, inputs, grad_cols)


def keep_kernel(slots_ref, keep_ref, residual_ref, column_ref, rows_ref):
    count = keep_ref.shape[1]
    row = lax.broadcasted_iota(jnp.int32, (count, count), 0)
    lane = lax.broadcasted_iota(jnp.int32, (count, count), 1)
    spread = jnp.where(row == lane, jnp.broadcast_to(keep_ref[...], (count, count)), 0)
    column = jnp.sum(spread.astype(jnp.float32), axis=1, keepdims=True)
    column_ref[...] = jnp.broadcast_to(column, column_ref.shape)

    def step(first, carry):
        for inner in range(8):
            index = first * 8 + inner
            rows_ref[pl.ds(index, 1), :] = residual_ref[pl.ds(slots_ref[0, index], 1), :]
        return carry

    lax.fori_loop(0, count // 8, step, 0)


def kept_part(region_keep, residual):
    count = region_keep.shape[1]
    vmem = pl.BlockSpec(memory_space=pltpu.VMEM)
    return pl.pallas_call(
        keep_kernel,
        out_shape=[jax.ShapeDtypeStruct((count, HEAD), jnp.float32)] * 2,
        in_specs=[pl.BlockSpec(memory_space=pltpu.SMEM), vmem, vmem],
        out_specs=[vmem, vmem],
        compiler_params=pltpu.CompilerParams(vmem_limit_bytes=8 * MIB),
        cost_estimate=pl.CostEstimate(flops=10**8, bytes_accessed=4 * MIB, transcendentals=0),
        name="kept_part",
    )(region_keep, region_keep, residual)


def split_rows(got_ref, parts_ref, offs_ref):
    stride = CAP + 1
    lane = lax.broadcasted_iota(jnp.int32, (1, LANES), 1)
    for pair in range(got_ref.shape[0] // stride // 2):
        first = 2 * pair * stride
        last = first + CAP
        offs_ref[:, pair * LANES : (pair + 1) * LANES] = jnp.where(
            lane < CAP, got_ref[last : last + 1], got_ref[last + stride : last + stride + 1]
        )
        for start, target in ((first, 2 * pair * CAP), (first + stride, (2 * pair + 1) * CAP)):
            values = got_ref[start : start + CAP]
            high = values.astype(jnp.bfloat16)
            low = (values - high.astype(jnp.float32)).astype(jnp.bfloat16)
            parts_ref[target : target + CAP, :HEAD] = high
            parts_ref[target : target + CAP, HEAD:] = low


def placed_sum(slots, offs_ref, parts_ref):
    place = jnp.concatenate(
        [
            jnp.where(slots == offs_ref[:, part : part + LANES], 1.0, 0.0).astype(jnp.bfloat16)
            for part in range(0, offs_ref.shape[1], LANES)
        ],
        axis=1,
    )
    summed = jnp.dot(place, parts_ref[...], preferred_element_type=jnp.float32)
    return summed[:, :HEAD] + summed[:, HEAD:]


def chosen_kernel(got_ref, column_ref, rows_ref, chosen_ref, parts_ref, offs_ref):
    split_rows(got_ref, parts_ref, offs_ref)
    chosen_ref[...] = placed_sum(column_ref[...], offs_ref, parts_ref) + rows_ref[...]


def part_scratch(got):
    filled = got.shape[0] // (CAP + 1) * CAP
    return [pltpu.VMEM((filled, 2 * HEAD), jnp.bfloat16), pltpu.VMEM((1, filled), jnp.float32)]


def chosen_totals(got, column, rows):
    vmem = pl.BlockSpec(memory_space=pltpu.VMEM)
    return pl.pallas_call(
        chosen_kernel,
        out_shape=jax.ShapeDtypeStruct(rows.shape, jnp.float32),
        in_specs=[vmem] * 3,
        out_specs=vmem,
        scratch_shapes=part_scratch(got),
        compiler_params=pltpu.CompilerParams(vmem_limit_bytes=16 * MIB),
        cost_estimate=pl.CostEstimate(flops=10**8, bytes_accessed=4 * MIB, transcendentals=0),
        name="chosen_totals",
    )(got, column, rows)


def refresh_kernel(length_ref, got_ref, keep_ref, residual_ref, out_ref, parts_ref, offs_ref):
    rows = out_ref.shape[0]
    base = pl.program_id(0) * rows
    length = length_ref[0]
    keep = keep_ref[...]

    @pl.when(base == 0)
    def _():
        split_rows(got_ref, parts_ref, offs_ref)

    for first in range(0, rows, SLOT_TILE):
        slot = lax.broadcasted_iota(jnp.int32, (SLOT_TILE, LANES), 0) + (base + first)
        hits = jnp.zeros((SLOT_TILE, LANES), jnp.float32)
        for part in range(0, keep.shape[1], LANES):
            hits = hits + jnp.where(slot == keep[:, part : part + LANES], 1.0, 0.0)
        named = jnp.sum(hits, axis=1, keepdims=True)
        survive = (slot < length) & (jnp.broadcast_to(named, slot.shape) == 0.0)
        summed = placed_sum(slot.astype(jnp.float32), offs_ref, parts_ref)
        totals = summed + residual_ref[first : first + SLOT_TILE]
        out_ref[first : first + SLOT_TILE] = jnp.where(survive, totals, 0.0)


def refreshed_slots(length, got, region_keep, residual, steps):
    slots = residual.shape[0]
    rows = slots // steps
    whole = lambda shape: pl.BlockSpec(shape, lambda i: (0, 0))
    return pl.pallas_call(
        refresh_kernel,
        out_shape=jax.ShapeDtypeStruct((slots, HEAD), jnp.float32),
        grid=(steps,),
        in_specs=[
            pl.BlockSpec(memory_space=pltpu.SMEM),
            pl.BlockSpec(memory_space=pltpu.VMEM),
            whole(region_keep.shape),
            pl.BlockSpec((rows, HEAD), lambda i: (i, 0)),
        ],
        out_specs=pl.BlockSpec((rows, HEAD), lambda i: (i, 0)),
        scratch_shapes=part_scratch(got),
        compiler_params=pltpu.CompilerParams(vmem_limit_bytes=24 * MIB),
        cost_estimate=pl.CostEstimate(flops=3 * 10**9, bytes_accessed=4 * MIB, transcendentals=0),
        name="refreshed_slots",
    )(length, got, region_keep, residual)


def body(activations, kv_grads, kept_blocks, region_bounds, region_keep, residual):
    inputs = activations[0, 0]
    grad_cols = kv_grads[0, 0]
    keep_count = kept_blocks.shape[3]
    residual = residual[0, 0]
    regions = lax.axis_size("rep")
    pods = lax.axis_size("outer")
    column_blocks = grad_cols.shape[1] // HEAD
    region_rows = residual.shape[0] // column_blocks
    owner = lax.axis_index("rep")
    length = (region_bounds[owner + 1] - region_bounds[owner]).reshape(1)

    sent = send_rows(region_bounds, kept_blocks.reshape(1, keep_count), inputs, grad_cols, region_rows)
    got = lax.all_to_all(
        sent.reshape(regions, CAP + 1, 1, HEAD),
        "rep",
        split_axis=0,
        concat_axis=0,
        tiled=True,
        axis_index_groups=[seating(regions)],
    ).reshape(regions * (CAP + 1), HEAD)
    pod_seats = list(range(pods - 1, -1, -1))
    seated_keep = region_keep.reshape(pods, -1)[::-1].reshape(region_keep.shape)
    column, rows = kept_part(seated_keep, residual)
    chosen = chosen_totals(got, column, rows)
    share = chosen.shape[0] // pods
    shares = lax.all_to_all(
        chosen.reshape(pods, share, HEAD),
        "outer",
        split_axis=0,
        concat_axis=0,
        tiled=True,
        axis_index_groups=[pod_seats],
    )
    merged = jnp.sum(shares, axis=0)
    refreshed = refreshed_slots(length, got, region_keep, residual, 3)
    return (merged[None], refreshed[None, None])


def solution(mesh):
    placed = (
        P("outer", "rep", None, None),
        P("outer", "rep", None, "tp"),
        P("outer", "rep", "tp", None),
        P(),
        P("rep", None),
        P("outer", "rep", None, "tp"),
    )
    return jax.shard_map(
        body,
        mesh=mesh,
        in_specs=placed,
        out_specs=(P("rep", "outer", "tp"), P("outer", "rep", None, "tp")),
        check_vma=False,
    )
```

```python
import functools

import jax
import jax.numpy as jnp
from jax import lax
from jax.experimental import pallas as pl
from jax.experimental.pallas import tpu as pltpu
from jax.sharding import PartitionSpec as P

HEAD = 128
CAP = 64
LANES = 128
SLOT_TILE = 256
BATCH = 8
MIB = 1 << 20
CONTRACT_LAST = (((1,), (1,)), ((), ()))


def contract_last(left, right):
    return lax.dot_general(left, right, CONTRACT_LAST, preferred_element_type=jnp.float32)


def seating(regions):
    return [seat ^ (regions - BATCH) for seat in range(regions)]


def send_kernel(
    region_rows, band, batch, bounds_hbm, ids_hbm, act_hbm, grad_hbm, out_hbm,
    bounds_ref, ids_ref, act_ref, grad_ref, out_ref, sems, out_sems,
):
    half = act_ref.shape[1] // 2
    loads = [
        pltpu.make_async_copy(source, target, sems.at[place])
        for place, (source, target) in enumerate(
            (
                (bounds_hbm, bounds_ref),
                (ids_hbm, ids_ref),
                (act_hbm.at[:, pl.ds(0, half)], act_ref.at[:, pl.ds(0, half)]),
                (grad_hbm, grad_ref),
                (act_hbm.at[:, pl.ds(half, half)], act_ref.at[:, pl.ds(half, half)]),
            )
        )
    ]
    for load in loads:
        load.start()
    loads[0].wait()
    loads[1].wait()
    regions = bounds_ref.shape[0] - 1
    keep_count = ids_ref.shape[1]
    width = act_ref.shape[1]
    column_blocks = grad_ref.shape[1] // HEAD
    column_bits = column_blocks.bit_length() - 1
    seats = seating(regions)
    chunks = keep_count // LANES
    stride = CAP + 1

    region_row = lax.broadcasted_iota(jnp.int32, (regions, LANES), 0)
    starts = jnp.zeros((regions, LANES), jnp.int32)
    ends = jnp.zeros((regions, LANES), jnp.int32)
    for region in range(regions):
        starts = jnp.where(region_row == region, bounds_ref[region], starts)
        ends = jnp.where(region_row == region, bounds_ref[region + 1], ends)

    ids = [ids_ref[:, c * LANES : (c + 1) * LANES] for c in range(chunks)]
    owned = [(i >= starts) & (i < ends) for i in ids]
    owned_f = [jnp.where(o, 1.0, 0.0) for o in owned]
    stacked = jnp.concatenate(owned_f, axis=0).astype(jnp.bfloat16)
    before = lax.broadcasted_iota(jnp.int32, (LANES, 2 * LANES), 0)
    after = lax.broadcasted_iota(jnp.int32, (LANES, 2 * LANES), 1)
    ladder = jnp.where((before < after) | (after >= LANES), 1.0, 0.0).astype(jnp.bfloat16)
    counted = jnp.dot(stacked, ladder, preferred_element_type=jnp.float32)
    running = jnp.zeros((regions, LANES), jnp.float32)
    rank_row = lax.broadcasted_iota(jnp.int32, (2 * CAP, LANES), 0) & (CAP - 1)
    ranked, high_part, low_part = [], [], []
    for c in range(chunks):
        rows = slice(c * regions, (c + 1) * regions)
        here = counted[rows, :LANES] + running
        running = running + counted[rows, LANES:]
        rank = jnp.sum(owned_f[c] * here, axis=0, keepdims=True).astype(jnp.int32)
        ranked.append(jnp.where(rank_row == rank, 1.0, 0.0).astype(jnp.bfloat16))
        code = ids[c] + 1
        high_part.append((owned_f[c] * (code >> 8).astype(jnp.float32)).astype(jnp.bfloat16))
        low_part.append((owned_f[c] * (code & 255).astype(jnp.float32)).astype(jnp.bfloat16))
    ranked = jnp.concatenate(ranked, axis=1)
    high_part = jnp.concatenate(high_part, axis=1)
    low_part = jnp.concatenate(low_part, axis=1)
    by_region = 256.0 * contract_last(high_part, ranked) + contract_last(low_part, ranked) - 1.0
    ranked = ranked[:CAP]
    by_rank = 256.0 * contract_last(ranked, high_part) + contract_last(ranked, low_part) - 1.0
    offsets = jnp.where(by_region < 0.0, -1.0, by_region - starts.astype(jnp.float32))

    lane = lax.broadcasted_iota(jnp.int32, (2 * CAP, LANES), 1)
    loads[3].wait()
    act_loads, waited = (loads[2], loads[4]), 0
    lane_low = lane.astype(jnp.bfloat16)
    paired = jnp.concatenate(
        [
            jnp.concatenate(
                [grad_ref[:, column * HEAD : (column + 1) * HEAD] for column in range(parity, column_blocks, 2)],
                axis=1,
            )
            for parity in range(2)
        ],
        axis=0,
    )
    held = []
    for first in range(0, regions, batch):
        columns, picked = [], []
        reach = min(width, (first + batch) * region_rows + band)
        while waited < len(act_loads) and reach > waited * half:
            act_loads[waited].wait()
            waited += 1
        for region in range(first, first + batch, 2):
            wanted = jnp.concatenate(
                [jnp.broadcast_to(by_rank[:, r : r + 1], (CAP, LANES)) for r in (region, region + 1)], axis=0
            ).astype(jnp.int32)
            base = (bounds_ref[region] >> column_bits) & ~(LANES - 1)
            base = pl.multiple_of(jnp.minimum(base, width - band), LANES)
            place = (wanted >> column_bits) - base
            columns.append(wanted & (column_blocks - 1))
            low = (place & (LANES - 1)).astype(jnp.bfloat16)
            high = (place >> 7).astype(jnp.bfloat16)
            zero = jnp.zeros(low.shape, jnp.bfloat16)
            one = jnp.ones(low.shape, jnp.bfloat16)
            hot = jnp.where(low == lane_low, high, zero - 1)
            chosen = jnp.concatenate(
                [jnp.where(hot == part, one, zero) for part in range(band // LANES)], axis=1
            )
            picked.append(contract_last(chosen, act_ref[:, pl.ds(base, band)]).astype(jnp.bfloat16))
        held.append((first, jnp.concatenate(columns, axis=0), jnp.concatenate(picked, axis=0)))

    stores = []
    for first, columns, rows in held:
        odd = (columns & 1).astype(jnp.bfloat16)
        zero = jnp.zeros_like(rows)
        spread = jnp.concatenate([jnp.where(odd == 0, rows, zero), jnp.where(odd == 0, zero, rows)], axis=1)
        wide = jnp.dot(spread, paired, preferred_element_type=jnp.float32)
        pair = columns >> 1
        block = wide[:, :HEAD]
        for place in range(1, column_blocks // 2):
            block = jnp.where(pair == place, wide[:, place * HEAD : (place + 1) * HEAD], block)
        for step in range(batch):
            region = first + step
            seat = seats.index(region)
            out_ref[seat * stride : seat * stride + CAP, :] = block[step * CAP : (step + 1) * CAP]
            out_ref[seat * stride + CAP : (seat + 1) * stride, :] = offsets[region : region + 1]
        block_first = min(seats.index(region) for region in range(first, first + batch))
        done = pl.ds(block_first * stride, batch * stride)
        store = pltpu.make_async_copy(out_ref.at[done], out_hbm.at[done], out_sems.at[first // batch])
        store.start()
        stores.append(store)
    for store in stores:
        store.wait()


def send_rows(region_bounds, block_ids, inputs, grad_cols, region_rows):
    regions = region_bounds.shape[0] - 1
    hbm = pl.BlockSpec(memory_space=pltpu.HBM)
    rows = regions * (CAP + 1)
    band = -(-(2 * region_rows + LANES) // (2 * LANES)) * (2 * LANES)
    return pl.pallas_call(
        functools.partial(send_kernel, region_rows, band, BATCH),
        out_shape=jax.ShapeDtypeStruct((rows, HEAD), jnp.float32),
        in_specs=[hbm] * 4,
        out_specs=hbm,
        scratch_shapes=[
            pltpu.SMEM(region_bounds.shape, jnp.int32),
            pltpu.VMEM(block_ids.shape, jnp.int32),
            pltpu.VMEM(inputs.shape, inputs.dtype),
            pltpu.VMEM(grad_cols.shape, grad_cols.dtype),
            pltpu.VMEM((rows, HEAD), jnp.float32),
            pltpu.SemaphoreType.DMA((5,)),
            pltpu.SemaphoreType.DMA((regions // BATCH,)),
        ],
        compiler_params=pltpu.CompilerParams(vmem_limit_bytes=62 * MIB),
        cost_estimate=pl.CostEstimate(flops=10**9, bytes_accessed=4 * MIB, transcendentals=0),
        name="send_rows",
    )(region_bounds, block_ids, inputs, grad_cols)


def keep_kernel(slots_ref, keep_ref, residual_ref, column_ref, rows_ref):
    count = keep_ref.shape[1]
    row = lax.broadcasted_iota(jnp.int32, (count, count), 0)
    lane = lax.broadcasted_iota(jnp.int32, (count, count), 1)
    spread = jnp.where(row == lane, jnp.broadcast_to(keep_ref[...], (count, count)), 0)
    column = jnp.sum(spread.astype(jnp.float32), axis=1, keepdims=True)
    column_ref[...] = jnp.broadcast_to(column, column_ref.shape)

    def step(first, carry):
        for inner in range(8):
            index = first * 8 + inner
            rows_ref[pl.ds(index, 1), :] = residual_ref[pl.ds(slots_ref[0, index], 1), :]
        return carry

    lax.fori_loop(0, count // 8, step, 0)


def kept_part(region_keep, residual):
    count = region_keep.shape[1]
    vmem = pl.BlockSpec(memory_space=pltpu.VMEM)
    return pl.pallas_call(
        keep_kernel,
        out_shape=[jax.ShapeDtypeStruct((count, HEAD), jnp.float32)] * 2,
        in_specs=[pl.BlockSpec(memory_space=pltpu.SMEM), vmem, vmem],
        out_specs=[vmem, vmem],
        compiler_params=pltpu.CompilerParams(vmem_limit_bytes=8 * MIB),
        cost_estimate=pl.CostEstimate(flops=10**8, bytes_accessed=4 * MIB, transcendentals=0),
        name="kept_part",
    )(region_keep, region_keep, residual)


def split_rows(got_ref, parts_ref, offs_ref):
    stride = CAP + 1
    lane = lax.broadcasted_iota(jnp.int32, (1, LANES), 1)
    for pair in range(got_ref.shape[0] // stride // 2):
        first = 2 * pair * stride
        last = first + CAP
        offs_ref[:, pair * LANES : (pair + 1) * LANES] = jnp.where(
            lane < CAP, got_ref[last : last + 1], got_ref[last + stride : last + stride + 1]
        )
        for start, target in ((first, 2 * pair * CAP), (first + stride, (2 * pair + 1) * CAP)):
            values = got_ref[start : start + CAP]
            high = values.astype(jnp.bfloat16)
            low = (values - high.astype(jnp.float32)).astype(jnp.bfloat16)
            parts_ref[target : target + CAP, :HEAD] = high
            parts_ref[target : target + CAP, HEAD:] = low


def placed_sum(slots, offs_ref, parts_ref):
    place = jnp.concatenate(
        [
            jnp.where(slots == offs_ref[:, part : part + LANES], 1.0, 0.0).astype(jnp.bfloat16)
            for part in range(0, offs_ref.shape[1], LANES)
        ],
        axis=1,
    )
    summed = jnp.dot(place, parts_ref[...], preferred_element_type=jnp.float32)
    return summed[:, :HEAD] + summed[:, HEAD:]


def chosen_kernel(got_ref, column_ref, rows_ref, chosen_ref, parts_ref, offs_ref):
    split_rows(got_ref, parts_ref, offs_ref)
    chosen_ref[...] = placed_sum(column_ref[...], offs_ref, parts_ref) + rows_ref[...]


def part_scratch(got):
    filled = got.shape[0] // (CAP + 1) * CAP
    return [pltpu.VMEM((filled, 2 * HEAD), jnp.bfloat16), pltpu.VMEM((1, filled), jnp.float32)]


def chosen_totals(got, column, rows):
    vmem = pl.BlockSpec(memory_space=pltpu.VMEM)
    return pl.pallas_call(
        chosen_kernel,
        out_shape=jax.ShapeDtypeStruct(rows.shape, jnp.float32),
        in_specs=[vmem] * 3,
        out_specs=vmem,
        scratch_shapes=part_scratch(got),
        compiler_params=pltpu.CompilerParams(vmem_limit_bytes=16 * MIB),
        cost_estimate=pl.CostEstimate(flops=10**8, bytes_accessed=4 * MIB, transcendentals=0),
        name="chosen_totals",
    )(got, column, rows)


def refresh_kernel(length_ref, got_ref, keep_ref, residual_ref, out_ref, parts_ref, offs_ref):
    rows = out_ref.shape[0]
    base = pl.program_id(0) * rows
    length = length_ref[0]
    keep = keep_ref[...]

    @pl.when(base == 0)
    def _():
        split_rows(got_ref, parts_ref, offs_ref)

    for first in range(0, rows, SLOT_TILE):
        slot = lax.broadcasted_iota(jnp.int32, (SLOT_TILE, LANES), 0) + (base + first)
        hits = jnp.zeros((SLOT_TILE, LANES), jnp.float32)
        for part in range(0, keep.shape[1], LANES):
            hits = hits + jnp.where(slot == keep[:, part : part + LANES], 1.0, 0.0)
        named = jnp.sum(hits, axis=1, keepdims=True)
        survive = (slot < length) & (jnp.broadcast_to(named, slot.shape) == 0.0)
        summed = placed_sum(slot.astype(jnp.float32), offs_ref, parts_ref)
        totals = summed + residual_ref[first : first + SLOT_TILE]
        out_ref[first : first + SLOT_TILE] = jnp.where(survive, totals, 0.0)


def refreshed_slots(length, got, region_keep, residual, steps):
    slots = residual.shape[0]
    rows = slots // steps
    whole = lambda shape: pl.BlockSpec(shape, lambda i: (0, 0))
    return pl.pallas_call(
        refresh_kernel,
        out_shape=jax.ShapeDtypeStruct((slots, HEAD), jnp.float32),
        grid=(steps,),
        in_specs=[
            pl.BlockSpec(memory_space=pltpu.SMEM),
            pl.BlockSpec(memory_space=pltpu.VMEM),
            whole(region_keep.shape),
            pl.BlockSpec((rows, HEAD), lambda i: (i, 0)),
        ],
        out_specs=pl.BlockSpec((rows, HEAD), lambda i: (i, 0)),
        scratch_shapes=part_scratch(got),
        compiler_params=pltpu.CompilerParams(vmem_limit_bytes=24 * MIB),
        cost_estimate=pl.CostEstimate(flops=3 * 10**9, bytes_accessed=4 * MIB, transcendentals=0),
        name="refreshed_slots",
    )(length, got, region_keep, residual)


def body(activations, kv_grads, kept_blocks, region_bounds, region_keep, residual):
    inputs = activations[0, 0]
    grad_cols = kv_grads[0, 0]
    keep_count = kept_blocks.shape[3]
    residual = residual[0, 0]
    regions = lax.axis_size("rep")
    pods = lax.axis_size("outer")
    column_blocks = grad_cols.shape[1] // HEAD
    region_rows = residual.shape[0] // column_blocks
    owner = lax.axis_index("rep")
    length = (region_bounds[owner + 1] - region_bounds[owner]).reshape(1)

    sent = send_rows(region_bounds, kept_blocks.reshape(1, keep_count), inputs, grad_cols, region_rows)
    got = lax.all_to_all(
        sent.reshape(regions, CAP + 1, 1, HEAD),
        "rep",
        split_axis=0,
        concat_axis=0,
        tiled=True,
        axis_index_groups=[seating(regions)],
    ).reshape(regions * (CAP + 1), HEAD)
    pod_seats = list(range(pods - 1, -1, -1))
    seated_keep = region_keep.reshape(pods, -1)[::-1].reshape(region_keep.shape)
    column, rows = kept_part(seated_keep, residual)
    chosen = chosen_totals(got, column, rows)
    share = chosen.shape[0] // pods
    shares = lax.all_to_all(
        chosen.reshape(pods, share, HEAD),
        "outer",
        split_axis=0,
        concat_axis=0,
        tiled=True,
        axis_index_groups=[pod_seats],
    )
    merged = jnp.sum(shares, axis=0)
    refreshed = refreshed_slots(length, got, region_keep, residual, 3)
    return (merged[None], refreshed[None, None])


def solution(mesh):
    placed = (
        P("outer", "rep", None, None),
        P("outer", "rep", None, "tp"),
        P("outer", "rep", "tp", None),
        P(),
        P("rep", None),
        P("outer", "rep", None, "tp"),
    )
    return jax.shard_map(
        body,
        mesh=mesh,
        in_specs=placed,
        out_specs=(P("rep", "outer", "tp"), P("outer", "rep", None, "tp")),
        check_vma=False,
    )
```
